32 devices in a mesh: gx: 2 (over core), gy: 4 (over z), gz: 4 (over y, x).
Axes of the slice: x: 2, y: 2, z: 4, core: 2. Of those that a mesh axis runs over, the one named last changes fastest.
Arguments:
- heat_source: float32 [32, 64, 512], P('gx', 'gy', 'gz'), may hold values from -6 to 6
- material: int32 [32, 64, 512], P('gx', 'gy', 'gz'), may hold values from 0 to 2
- conductivity: float32 [3], replicated, may hold values from 0.3 to 3
Outputs:
- temperature: float32 [32, 64, 512], P('gx', 'gy', 'gz')
The draws below stay inside these ranges and needn't reach their ends.
All inputs are finite; a program needn't handle non-finite values.
Results may differ from the reference program's by a relative error of at most 0.00002.
Values sent between devices are 32-bit elements; how exact they have to be, the bound alone decides.
A program may use at most 192 MiB of HBM per device.

```python
import math
import jax
import jax.numpy as jnp

DEGREE = 3
LEVELS = 3
MATERIALS = 3
NX = 32
NY = 64
NZ = 512


def plant(result, rng, low, top_value):
    shape = result.shape
    place = [jax.random.randint(jax.random.fold_in(rng, axis), (), 0, shape[axis]) for axis in range(len(shape))]
    result = result.at[tuple(place)].set(low)
    longest = shape.index(max(shape))
    place[longest] = (place[longest] + 1) % shape[longest]
    return result.at[tuple(place)].set(top_value)


def levels(own_key, extent, pieces, least, largest):
    gain, own = 1.0, jax.random.fold_in(own_key, 6)
    for dim, blocks in pieces:
        steps = jnp.exp(jax.random.uniform(jax.random.fold_in(own, dim), (blocks,), jnp.float32, least / len(pieces), largest / len(pieces)))
        gain = gain * jnp.repeat(steps, extent[dim] // blocks).reshape([-1 if axis == dim else 1 for axis in range(len(extent))])
    return gain


def bell_draw(key, dims, scale, most, cuts=(), dtype=jnp.bfloat16):
    level = levels(key, dims, cuts, -0.22, 0.18) if cuts else 1.0
    entries = jax.random.normal(key, dims, jnp.float32) * scale * level
    return jnp.minimum(jnp.maximum(entries, -most), most).astype(dtype)


def setup_inputs(seed: int = 0) -> dict:
    arg_keys = jax.random.split(jax.random.key(seed), 4)
    heat_source = bell_draw(arg_keys[0], (NX, NY, NZ), 1.0, 6.0, ((0, 2), (1, 4), (2, 4)), jnp.float32)
    material = plant(jax.random.randint(arg_keys[1], (NX, NY, NZ), 0, 3), jax.random.fold_in(arg_keys[1], 1), 0, 2).astype(jnp.int32)
    conductivity = jnp.clip(jnp.exp(jax.random.uniform(arg_keys[2], (MATERIALS,), jnp.float32, math.log(0.3), math.log(3.0))), 0.3, 3.0)
    return {"heat_source": heat_source, "material": material, "conductivity": conductivity}


LOW = 0.3
HIGH = 2.0


def harmonic(left, right):
    return 2.0 * left * right / (left + right)


def neighbours(padded):
    return (padded[2:, 1:-1, 1:-1], padded[:-2, 1:-1, 1:-1], padded[1:-1, 2:, 1:-1],
            padded[1:-1, :-2, 1:-1], padded[1:-1, 1:-1, 2:], padded[1:-1, 1:-1, :-2])


def face_set(cond):
    padded = jnp.pad(cond, 1, mode="edge")
    faces = tuple(harmonic(cond, other) for other in neighbours(padded))
    diag = faces[0] + faces[1] + faces[2] + faces[3] + faces[4] + faces[5]
    return faces, diag


def operate(field, faces, diag, scale):
    near = neighbours(jnp.pad(field, 1))
    total = faces[0] * near[0] + faces[1] * near[1] + faces[2] * near[2]
    total = total + faces[3] * near[3] + faces[4] * near[4] + faces[5] * near[5]
    return scale * (diag * field - total)


def smooth(right, start, faces, diag, scale):
    theta = 0.5 * (HIGH + LOW)
    delta = 0.5 * (HIGH - LOW)
    sigma = theta / delta
    rho = 1.0 / sigma
    inverse = 1.0 / (scale * diag)
    if start is None:
        resid = right
        step_dir = inverse * resid / theta
        field = step_dir
    else:
        resid = right - operate(start, faces, diag, scale)
        step_dir = inverse * resid / theta
        field = start + step_dir
    for turn in range(DEGREE - 1):
        rho_new = 1.0 / (2.0 * sigma - rho)
        resid = right - operate(field, faces, diag, scale)
        step_dir = rho_new * rho * step_dir + (2.0 * rho_new / delta) * inverse * resid
        field = field + step_dir
        rho = rho_new
    return field


def restrict(field):
    sx, sy, sz = field.shape
    return field.reshape(sx // 2, 2, sy // 2, 2, sz // 2, 2).mean(axis=(1, 3, 5))


def prolong(field):
    return jnp.repeat(jnp.repeat(jnp.repeat(field, 2, 0), 2, 1), 2, 2)


def cycle(right, cond, level, scale):
    faces, diag = face_set(cond)
    if level == LEVELS:
        field = smooth(right, None, faces, diag, scale)
        return smooth(right, field, faces, diag, scale)
    field = smooth(right, None, faces, diag, scale)
    resid = right - operate(field, faces, diag, scale)
    error = cycle(restrict(resid), restrict(cond), level + 1, scale * 0.25)
    field = field + prolong(error)
    return smooth(right, field, faces, diag, scale)


def reference(heat_source, material, conductivity):
    cond = jnp.zeros(heat_source.shape, jnp.float32)
    for which in range(MATERIALS):
        cond = cond + jnp.where(material == which, conductivity[which], jnp.float32(0.0))
    return cycle(heat_source, cond, 0, 1.0)
```

```python
import functools

import jax
import jax.numpy as jnp
from jax import lax
from jax.experimental import pallas as pl
from jax.experimental.pallas import tpu as pltpu
from jax.sharding import PartitionSpec as P

DEGREE = 3
LEVELS = 3
MATERIALS = 3

LOW = 0.3
HIGH = 2.0
THETA = 0.5 * (HIGH + LOW)
DELTA = 0.5 * (HIGH - LOW)
SIGMA = THETA / DELTA

HX = 6
HY = 8
HZ = 8
MESH = pl.DeviceIdType.MESH
F32 = jnp.float32


def chebyshev():
    rho = 1.0 / SIGMA
    pairs = []
    for _ in range(DEGREE - 1):
        new = 1.0 / (2.0 * SIGMA - rho)
        pairs.append((new * rho, 2.0 * new / DELTA))
        rho = new
    return pairs


def up(v, axis):
    return pltpu.roll(v, v.shape[axis] - 1, axis)


def down(v, axis):
    return pltpu.roll(v, 1, axis)


def harmonic(a, b):
    return jnp.where((a > 0.0) & (b > 0.0), 2.0 * a * b / (a + b), 0.0)


def build(cond, n, faces_x, faces_y, faces_z, edge, inverse, scale, ring=False):
    shape = cond.shape[1:]
    row = lax.broadcasted_iota(jnp.int32, shape, 0)
    lane = lax.broadcasted_iota(jnp.int32, shape, 1)

    def plane(i, k, k_low, k_high, fx_low):
        ky_high = jnp.where(row == shape[0] - 1, 0.0, up(k, 0))
        ky_low = jnp.where(row == 0, 0.0, down(k, 0))
        kz_high, kz_low = up(k, 1), down(k, 1)
        if not ring:
            kz_high = jnp.where(lane == shape[1] - 1, 0.0, kz_high)
            kz_low = jnp.where(lane == 0, 0.0, kz_low)
        fx, fy, fz = harmonic(k, k_high), harmonic(k, ky_high), harmonic(k, kz_high)
        missing = jnp.zeros(shape, F32)
        for other in (k_low, k_high, ky_low, ky_high, kz_low, kz_high):
            missing = missing + jnp.where(other > 0.0, 0.0, k)
        diag = fx + fx_low + fy + down(fy, 0) + fz + down(fz, 1) + missing
        faces_x[i] = fx
        faces_y[i] = fy
        faces_z[i] = fz
        edge[i] = missing
        inverse[i] = jnp.where(k > 0.0, 1.0 / (scale * diag), 0.0)
        return fx

    def body(i, carry):
        k, k_low, fx_low = carry
        k_high = cond[i + 1]
        fx = plane(i, k, k_low, k_high, fx_low)
        return k_high, k, fx

    zero = jnp.zeros(shape, F32)
    k, k_low, fx_low = lax.fori_loop(0, n - 1, body, (cond[0], zero, zero))
    plane(n - 1, k, k_low, zero, fx_low)


def first(n, right, inverse, field, step):
    def body(i, _):
        value = inverse[i] * right[i] * (1.0 / THETA)
        field[i] = value
        step[i] = value
        return 0

    lax.fori_loop(0, n, body, 0)


def residuals(lo, hi, right, field, coefs, scale, use):
    faces_x, faces_y, faces_z, edge = coefs[:4]

    def body(i, carry):
        x, flux_low = carry
        x_high = field[i + 1]
        flux = faces_x[i] * (x_high - x)
        flux_y = faces_y[i] * (up(x, 0) - x)
        flux_z = faces_z[i] * (up(x, 1) - x)
        total = (flux - flux_low) + (flux_y - down(flux_y, 0)) + (flux_z - down(flux_z, 1))
        total = total - edge[i] * x
        use(i, x, right[i] + scale * total)
        return x_high, flux

    x = field[lo]
    low = faces_x[lo - 1] * (x - field[lo - 1]) if lo > 0 else jnp.zeros(x.shape, F32)
    lax.fori_loop(lo, hi, body, (x, low), unroll=2)


def sweep(lo, hi, right, field, step, coefs, scale, keep, gain):
    inverse = coefs[4]

    def use(i, x, resid):
        d = gain * (inverse[i] * resid)
        if keep is not None:
            d = d + keep * step[i]
        step[i] = d
        field[i] = x + d

    residuals(lo, hi, right, field, coefs, scale, use)


def pairs_rows(out_rows, in_rows):
    r = lax.broadcasted_iota(jnp.int32, (out_rows, in_rows), 0)
    c = lax.broadcasted_iota(jnp.int32, (out_rows, in_rows), 1)
    return jnp.where((c == 2 * r) | (c == 2 * r + 1), 1.0, 0.0).astype(F32)


def pairs_lanes(in_lanes, out_lanes, shift=0):
    r = lax.broadcasted_iota(jnp.int32, (in_lanes, out_lanes), 0)
    c = lax.broadcasted_iota(jnp.int32, (in_lanes, out_lanes), 1) - shift
    return jnp.where((r == 2 * c) | (r == 2 * c + 1), 1.0, 0.0).astype(F32)


def dot(a, b):
    return jnp.dot(a, b, precision=lax.Precision.HIGHEST, preferred_element_type=F32)


def full_smooth(n, right, field, step, coefs, scale, zero_start):
    if zero_start:
        first(n, right, coefs[4], field, step)
    else:
        sweep(0, n, right, field, step, coefs, scale, None, 1.0 / THETA)
    for keep, gain in chebyshev():
        sweep(0, n, right, field, step, coefs, scale, keep, gain)


def coarse_cycle(levels, level):
    n, cond, right, field, step, coefs, temp, scale = levels[level]
    build(cond, n, *coefs, scale)
    field[n] = jnp.zeros(field.shape[1:], F32)
    full_smooth(n, right, field, step, coefs, scale, True)
    if level == len(levels) - 1:
        full_smooth(n, right, field, step, coefs, scale, False)
        return
    half, below, below_right, below_field = n // 2, *levels[level + 1][1:4]
    rows, lanes = field.shape[1:]
    out_rows, out_lanes = below_field.shape[1:]

    def keep_resid(i, x, resid):
        temp[i] = resid

    residuals(0, n, right, field, coefs, scale, keep_resid)
    merge = pairs_rows(half * out_rows, half * rows)
    squeeze = pairs_lanes(lanes, out_lanes)
    for source, target in ((temp, below_right), (cond, below)):
        both = source[...].reshape(half, 2, rows, lanes)
        both = (both[:, 0] + both[:, 1]).reshape(half * rows, lanes)
        target[...] = (dot(dot(merge, both), squeeze) * 0.125).reshape(half, out_rows, out_lanes)
    coarse_cycle(levels, level + 1)
    error = below_field[pl.ds(0, half)].reshape(half * out_rows, out_lanes)
    split = lax.broadcasted_iota(jnp.int32, (half * rows, half * out_rows), 0) // 2
    split = jnp.where(
        split == lax.broadcasted_iota(jnp.int32, (half * rows, half * out_rows), 1), 1.0, 0.0
    )
    spread = lax.broadcasted_iota(jnp.int32, (out_lanes, lanes), 1) // 2
    spread = jnp.where(
        spread == lax.broadcasted_iota(jnp.int32, (out_lanes, lanes), 0), 1.0, 0.0
    )
    error = dot(dot(split, error), spread).reshape(half, rows, lanes)
    for i in range(half):
        field[2 * i] = field[2 * i] + error[i]
        field[2 * i + 1] = field[2 * i + 1] + error[i]
    full_smooth(n, right, field, step, coefs, scale, False)


def halo_kernel(sizes, heat, material, table, ext, pack, got, sems_out, sems_in):
    nx, ny, nz = sizes
    ix, iy, iz = lax.axis_index("gx"), lax.axis_index("gy"), lax.axis_index("gz")
    bx, by, bz = heat.shape
    ext[...] = jnp.zeros(ext.shape, F32)
    got[...] = jnp.zeros(got.shape, F32)
    own = (pl.ds(HX, bx), pl.ds(HY, by), pl.ds(0, bz))
    ext[(0, *own)] = heat[...]
    cond = jnp.zeros(heat.shape, F32)
    for which in range(MATERIALS):
        cond = cond + jnp.where(material[...] == which, table[which], 0.0)
    ext[(1, *own)] = cond

    sides = []
    for axis, at, count in (("gx", ix, nx), ("gy", iy, ny), ("gz", iz, nz)):
        sides.append((axis, at > 0, at - 1))
        sides.append((axis, at < count - 1, at + 1))

    barrier = pltpu.get_barrier_semaphore()
    for axis, there, other in sides:
        @pl.when(there)
        def _():
            pl.semaphore_signal(barrier, inc=1, device_id={axis: other}, device_id_type=MESH)
    pl.semaphore_wait(barrier, sum(jnp.where(there, 1, 0) for _, there, _ in sides))

    def exchange(which, low_source, low_target, high_source, high_target):
        copies = []
        for turn, (source, target) in enumerate(
            ((low_source, low_target), (high_source, high_target))
        ):
            axis, there, other = sides[which + turn]
            copy = pltpu.make_async_remote_copy(
                src_ref=source,
                dst_ref=target,
                send_sem=sems_out.at[which + turn],
                recv_sem=sems_in.at[which + turn],
                device_id={axis: other},
                device_id_type=MESH,
            )
            copies.append((there, copy))
            pl.when(there)(copy.start)
        pl.when(copies[0][0])(copies[1][1].wait_recv)
        pl.when(copies[1][0])(copies[0][1].wait_recv)
        pl.when(copies[0][0])(copies[0][1].wait_send)
        pl.when(copies[1][0])(copies[1][1].wait_send)

    def rows(start):
        return ext.at[:, pl.ds(HX, bx), pl.ds(start, HY), pl.ds(0, bz)]

    exchange(2, rows(HY), rows(HY + by), rows(by), rows(0))

    lane = lax.broadcasted_iota(jnp.int32, (ext.shape[2], bz), 1)
    for part in range(2):
        low = jnp.zeros((ext.shape[2], bz), F32)
        high = low
        for x in range(bx):
            v = ext[part, HX + x, :, pl.ds(0, bz)]
            mine = (lane >= HZ * x) & (lane < HZ * (x + 1))
            low = jnp.where(mine, pltpu.roll(v, (HZ * x) % bz, 1), low)
            high = jnp.where(mine, pltpu.roll(v, HZ * (x + 1) % bz, 1), high)
        pack[0, part] = low
        pack[1, part] = high
    exchange(4, pack.at[0], got.at[1], pack.at[1], got.at[0])
    for part in range(2):
        left, right = got[0, part], got[1, part]
        for x in range(bx):
            v = jnp.where(lane < HZ, pltpu.roll(right, (bz - HZ * x) % bz, 1), 0.0)
            v = jnp.where(lane >= bz - HZ, pltpu.roll(left, (2 * bz - HZ * (x + 1)) % bz, 1), v)
            ext[part, HX + x, :, pl.ds(bz, bz)] = v

    def planes(start):
        return ext.at[:, pl.ds(start, HX)]

    exchange(0, planes(HX), planes(HX + bx), planes(bx), planes(0))


def pre_kernel(ext, field, packed, fx, fy, fz, edge, inverse, step, temp):
    n = ext.shape[1]
    bx, by, bz = n - 2 * HX, ext.shape[2] - 2 * HY, ext.shape[3] // 2
    right, cond = ext.at[0], ext.at[1]
    coefs = (fx, fy, fz, edge, inverse)
    build(cond, n, *coefs, 1.0, True)
    first(n, right, inverse, field, step)
    for turn, (keep, gain) in enumerate(chebyshev()):
        sweep(2 + turn, n - 2 - turn, right, field, step, coefs, 1.0, keep, gain)

    def keep_resid(i, x, resid):
        temp[i - HX] = resid[HY:HY + by, :bz]

    residuals(HX, HX + bx, right, field, coefs, 1.0, keep_resid)
    merge = pairs_rows(bx // 2 * by // 2, bx // 2 * by)
    result = jnp.zeros((bx // 2 * by // 2, bz), F32)
    for shift, source in (
        (0, temp[...]),
        (bz // 2, cond[pl.ds(HX, bx), pl.ds(HY, by), pl.ds(0, bz)]),
    ):
        both = source.reshape(bx // 2, 2, by, bz)
        both = (both[:, 0] + both[:, 1]).reshape(bx // 2 * by, bz)
        squeeze = pairs_lanes(bz, bz, shift)
        if shift == 0:
            lane = lax.broadcasted_iota(jnp.int32, (bz, bz), 1)
            squeeze = jnp.where(lane < bz // 2, squeeze, 0.0)
        result = result + dot(dot(merge, both), squeeze)
    packed[...] = (result * 0.125).reshape(bx // 2, by // 2, bz)


def gather_kernel(sizes, block, full, sems_out, sems_in):
    nx, ny, nz = sizes
    ix, iy, iz = lax.axis_index("gx"), lax.axis_index("gy"), lax.axis_index("gz")
    partners = []
    for axis, at, count in (("gy", iy, ny), ("gz", iz, nz), ("gx", ix, nx)):
        partners.append([(axis, lax.rem(at + off, count)) for off in range(1, count)])
    full[ix, iz, iy] = block[...]
    barrier = pltpu.get_barrier_semaphore()
    total = 0
    for group in partners:
        for axis, other in group:
            pl.semaphore_signal(barrier, inc=1, device_id={axis: other}, device_id_type=MESH)
            total += 1
    pl.semaphore_wait(barrier, total)
    slot = 0
    sent = []
    for group, source in zip(partners, (full.at[ix, iz, iy], full.at[ix, iz], full.at[ix])):
        copies = []
        for axis, other in group:
            copy = pltpu.make_async_remote_copy(
                src_ref=source,
                dst_ref=source,
                send_sem=sems_out.at[slot],
                recv_sem=sems_in.at[slot],
                device_id={axis: other},
                device_id_type=MESH,
            )
            copy.start()
            copies.append(copy)
            slot += 1
        for copy in copies:
            copy.wait_recv()
        sent += copies
    for copy in sent:
        copy.wait_send()


def post_kernel(sizes, ext, start, full, out, *scratch):
    nx, ny, nz = sizes
    ix, iy, iz = lax.axis_index("gx"), lax.axis_index("gy"), lax.axis_index("gz")
    n = ext.shape[1]
    bx, by, bz = out.shape
    scratch = list(scratch)
    field, step, *coefs = scratch[:7]
    levels, place, scale = [], 7, 0.25
    pad = HX // 2
    for level in range(1, LEVELS + 1):
        cond, right, whole, moves, temp, *five = scratch[place:place + 10]
        place += 10
        planes = cond.shape[0]
        values = whole.at[pl.ds(pad, planes + 1)] if level == 1 else whole
        if level == 1:
            coarse = whole
        levels.append((planes, cond, right, values, moves, tuple(five), temp, scale))
        scale *= 0.25
    _, cond, right = levels[0][:3]

    cx, cy = bx // 2, by // 2
    lane = lax.broadcasted_iota(jnp.int32, (cy, bz), 1)

    def assemble(i, _):
        for px in range(nx):
            for q in range(nz // 2):
                for py in range(ny):
                    one, two = full[px, 2 * q, py, i], full[px, 2 * q + 1, py, i]
                    where = (px * cx + i, pl.ds(py * cy, cy), pl.ds(q * bz, bz))
                    right[where] = jnp.where(lane < bz // 2, one, pltpu.roll(two, bz // 2, 1))
                    cond[where] = jnp.where(lane < bz // 2, pltpu.roll(one, bz // 2, 1), two)
        return 0

    lax.fori_loop(0, cx, assemble, 0)
    zero = jnp.zeros((pad, *coarse.shape[1:]), F32)
    coarse[pl.ds(0, pad)] = zero
    coarse[pl.ds(coarse.shape[0] - pad, pad)] = zero
    coarse_cycle(levels, 0)

    rows, lanes = ext.shape[2:]
    crows, clanes = coarse.shape[1:]
    r = lax.broadcasted_iota(jnp.int32, (rows, crows), 0)
    c = lax.broadcasted_iota(jnp.int32, (rows, crows), 1)
    fine = 2 * (c - cy * iy) + HY
    split = jnp.where((r == fine) | (r == fine + 1), 1.0, 0.0).astype(F32)
    r = lax.broadcasted_iota(jnp.int32, (clanes, lanes), 0)
    c = lax.broadcasted_iota(jnp.int32, (clanes, lanes), 1)
    c = jnp.where(c >= lanes - HZ, c - lanes, c)
    fine = 2 * (r - bz // 2 * iz)
    spread = jnp.where((c == fine) | (c == fine + 1), 1.0, 0.0).astype(F32)

    build(ext.at[1], n, *coefs, 1.0, True)
    window = coarse[pl.ds(cx * ix, n // 2)].reshape(n // 2 * crows, clanes)
    window = dot(window, spread).reshape(n // 2, crows, lanes)
    for i in range(n // 2):
        error = dot(split, window[i])
        field[2 * i] = start[2 * i] + error
        field[2 * i + 1] = start[2 * i + 1] + error
    right = ext.at[0]
    sweep(HX - 2, n - HX + 2, right, field, step, coefs, 1.0, None, 1.0 / THETA)
    for turn, (keep, gain) in enumerate(chebyshev()):
        low = HX - 1 + turn
        sweep(low, n - low, right, field, step, coefs, 1.0, keep, gain)
    for i in range(bx):
        out[i] = field[HX + i, HY:HY + by, :bz]


def local(sizes, heat, material, table):
    nx, ny, nz = sizes
    bx, by, bz = heat.shape
    n, rows, lanes = bx + 2 * HX, by + 2 * HY, 2 * bz
    vmem = pl.BlockSpec(memory_space=pltpu.VMEM)
    smem = pl.BlockSpec(memory_space=pltpu.SMEM)
    limit = 48 * 1024 * 1024
    array = jax.ShapeDtypeStruct
    ext = pl.pallas_call(
        functools.partial(halo_kernel, sizes),
        out_shape=array((2, n, rows, lanes), F32),
        in_specs=[vmem, vmem, smem],
        out_specs=vmem,
        scratch_shapes=[
            pltpu.VMEM((2, 2, rows, bz), F32),
            pltpu.VMEM((2, 2, rows, bz), F32),
            pltpu.SemaphoreType.DMA((6,)),
            pltpu.SemaphoreType.DMA((6,)),
        ],
        compiler_params=pltpu.CompilerParams(
            collective_id=0, has_side_effects=True, vmem_limit_bytes=limit
        ),
    )(heat, material, table)
    fine = pltpu.VMEM((n, rows, lanes), F32)
    start, packed = pl.pallas_call(
        pre_kernel,
        out_shape=[array((n, rows, lanes), F32), array((bx // 2, by // 2, bz), F32)],
        in_specs=[vmem],
        out_specs=[vmem, vmem],
        scratch_shapes=[fine] * 6 + [pltpu.VMEM((bx, by, bz), F32)],
        compiler_params=pltpu.CompilerParams(vmem_limit_bytes=limit),
    )(ext)
    count = nx + ny + nz - 3
    full = pl.pallas_call(
        functools.partial(gather_kernel, sizes),
        out_shape=array((nx, nz, ny, bx // 2, by // 2, bz), F32),
        in_specs=[vmem],
        out_specs=vmem,
        scratch_shapes=[pltpu.SemaphoreType.DMA((count,)), pltpu.SemaphoreType.DMA((count,))],
        compiler_params=pltpu.CompilerParams(
            collective_id=1, has_side_effects=True, vmem_limit_bytes=limit
        ),
    )(packed)
    scratch = [fine] * 7
    for level in range(1, LEVELS + 1):
        shape = (bx * nx >> level, by * ny >> level, max(bz * nz >> level, 128))
        extra = HX if level == 1 else 1
        scratch += [pltpu.VMEM(shape, F32)] * 2
        scratch += [pltpu.VMEM((shape[0] + extra, *shape[1:]), F32)]
        scratch += [pltpu.VMEM(shape, F32)] * 7
    return pl.pallas_call(
        functools.partial(post_kernel, sizes),
        out_shape=array(heat.shape, F32),
        in_specs=[vmem] * 3,
        out_specs=vmem,
        scratch_shapes=scratch,
        compiler_params=pltpu.CompilerParams(vmem_limit_bytes=limit),
    )(ext, start, full)


def with_halo(block, sides):
    for axis, dim in sides:
        count = lax.axis_size(axis)
        forward = [(i, i + 1) for i in range(count - 1)]
        backward = [(target, source) for source, target in forward]
        low = lax.ppermute(
            lax.slice_in_dim(block, block.shape[dim] - 1, None, axis=dim), axis, forward
        )
        high = lax.ppermute(lax.slice_in_dim(block, 0, 1, axis=dim), axis, backward)
        block = jnp.concatenate([low, block, high], axis=dim)
    return block


def neighbours(block):
    padded = with_halo(block, (("gx", 0), ("gy", 1), ("gz", 2)))
    return (
        padded[2:, 1:-1, 1:-1],
        padded[:-2, 1:-1, 1:-1],
        padded[1:-1, 2:, 1:-1],
        padded[1:-1, :-2, 1:-1],
        padded[1:-1, 1:-1, 2:],
        padded[1:-1, 1:-1, :-2],
    )


def large_smooth(right, start, faces, diag, scale):
    inverse = 1.0 / (scale * diag)
    if start is None:
        step = inverse * right / THETA
        field = step
    else:
        step = inverse * large_resid(right, start, faces, diag, scale) / THETA
        field = start + step
    for keep, gain in chebyshev():
        step = keep * step + gain * inverse * large_resid(right, field, faces, diag, scale)
        field = field + step
    return field


def large_resid(right, field, faces, diag, scale):
    total = sum(face * near for face, near in zip(faces, neighbours(field)))
    return right - scale * (diag * field - total)


def restrict(field):
    sx, sy, sz = field.shape
    return field.reshape(sx // 2, 2, sy // 2, 2, sz // 2, 2).mean(axis=(1, 3, 5))


def large_cycle(right, cond, level, scale):
    faces = []
    for other in neighbours(cond):
        other = jnp.where(other > 0.0, other, cond)
        faces.append(2.0 * cond * other / (cond + other))
    diag = sum(faces)
    field = large_smooth(right, None, faces, diag, scale)
    if level < LEVELS:
        resid = large_resid(right, field, faces, diag, scale)
        error = large_cycle(restrict(resid), restrict(cond), level + 1, scale * 0.25)
        for dim in range(3):
            error = jnp.repeat(error, 2, dim)
        field = field + error
    return large_smooth(right, field, faces, diag, scale)


def large(heat, material, table):
    cond = jnp.zeros(heat.shape, F32)
    for which in range(MATERIALS):
        cond = cond + jnp.where(material == which, table[which], 0.0)
    return large_cycle(heat, cond, 0, 1.0)


def solution(mesh):
    sizes = tuple(mesh.shape[axis] for axis in ("gx", "gy", "gz"))

    def run(heat, material, table):
        small = heat.size // 8 <= 1 << 18
        body = functools.partial(local, sizes) if small else large
        spec = P("gx", "gy", "gz")
        return jax.shard_map(
            body, mesh=mesh, in_specs=(spec, spec, P()), out_specs=spec, check_vma=False
        )(heat, material, table)

    return run
```

```python
import functools

import jax
import jax.numpy as jnp
from jax import lax
from jax.experimental import pallas as pl
from jax.experimental.pallas import tpu as pltpu
from jax.sharding import PartitionSpec as P

DEGREE = 3
LEVELS = 3
MATERIALS = 3

LOW = 0.3
HIGH = 2.0
THETA = 0.5 * (HIGH + LOW)
DELTA = 0.5 * (HIGH - LOW)
SIGMA = THETA / DELTA

HX = 6
HY = 8
HZ = 8
MESH = pl.DeviceIdType.MESH
F32 = jnp.float32


def chebyshev():
    rho = 1.0 / SIGMA
    pairs = []
    for _ in range(DEGREE - 1):
        new = 1.0 / (2.0 * SIGMA - rho)
        pairs.append((new * rho, 2.0 * new / DELTA))
        rho = new
    return pairs


def up(v, axis):
    return pltpu.roll(v, v.shape[axis] - 1, axis)


def down(v, axis):
    return pltpu.roll(v, 1, axis)


def harmonic(a, b):
    return 2.0 * a * b / jnp.maximum(a + b, 1e-30)


def build(cond, n, right, coefs, field, step, scale, ring=False):
    faces, over, diagonal = coefs
    shape = cond.shape[1:]
    row = lax.broadcasted_iota(jnp.int32, shape, 0)
    lane = lax.broadcasted_iota(jnp.int32, shape, 1)

    def plane(i, k, k_low, k_high, fx_low):
        ky_high = jnp.where(row == shape[0] - 1, 0.0, up(k, 0))
        ky_low = jnp.where(row == 0, 0.0, down(k, 0))
        kz_high, kz_low = up(k, 1), down(k, 1)
        if not ring:
            kz_high = jnp.where(lane == shape[1] - 1, 0.0, kz_high)
            kz_low = jnp.where(lane == 0, 0.0, kz_low)
        fx, fy, fz = harmonic(k, k_high), harmonic(k, ky_high), harmonic(k, kz_high)
        missing = jnp.zeros(shape, F32)
        for other in (k_low, k_high, ky_low, ky_high, kz_low, kz_high):
            missing = missing + jnp.where(other > 0.0, 0.0, k)
        fy_low, fz_low = down(fy, 0), down(fz, 1)
        diag = fx + fx_low + fy + fy_low + fz + fz_low + missing
        inverse = jnp.where(k > 0.0, 1.0 / jnp.maximum(diag, 1e-30), 0.0)
        for side, face in enumerate((fx, fx_low, fy, fy_low, fz, fz_low)):
            faces[side, i] = face * inverse
        value = inverse * (1.0 / scale) * right[i]
        over[i] = value
        diagonal[i] = diag * scale
        field[i] = value * (1.0 / THETA)
        step[i] = value * (1.0 / THETA)
        return fx

    def body(i, carry):
        k, k_low, fx_low = carry
        k_high = cond[i + 1]
        fx = plane(i, k, k_low, k_high, fx_low)
        return k_high, k, fx

    zero = jnp.zeros(shape, F32)
    unroll = True if n <= 8 else 3
    k, k_low, fx_low = lax.fori_loop(0, n - 1, body, (cond[0], zero, zero), unroll=unroll)
    plane(n - 1, k, k_low, zero, fx_low)


def residuals(lo, hi, field, coefs, use):
    faces, over = coefs[:2]
    group = min(hi - lo, 8 if field.shape[1] <= 16 else 4)

    def body(turn, carry):
        start = lo + turn * group
        xs = list(carry) + [field[start + j + 1] for j in range(group)]
        results = []
        for j in range(group):
            i, x = start + j, xs[j + 1]
            along_x = faces[0, i] * xs[j + 2] + faces[1, i] * xs[j]
            along_y = faces[2, i] * up(x, 0) + faces[3, i] * down(x, 0)
            along_z = faces[4, i] * up(x, 1) + faces[5, i] * down(x, 1)
            results.append(((over[i] - x) + along_x) + (along_y + along_z))
        use(start, xs[1:-1], results)
        return xs[-2], xs[-1]

    low = field[lo - 1] if lo > 0 else jnp.zeros(field.shape[1:], F32)
    lax.fori_loop(0, (hi - lo) // group, body, (low, field[lo]))


def sweep(lo, hi, field, step, coefs, keep, gain):
    def use(start, xs, results):
        moves = [gain * z for z in results]
        if keep is not None:
            moves = [keep * step[start + j] + move for j, move in enumerate(moves)]
        for j, (x, move) in enumerate(zip(xs, moves)):
            step[start + j] = move
            field[start + j] = x + move

    residuals(lo, hi, field, coefs, use)


def pairs_rows(out_rows, in_rows):
    r = lax.broadcasted_iota(jnp.int32, (out_rows, in_rows), 0)
    c = lax.broadcasted_iota(jnp.int32, (out_rows, in_rows), 1)
    return jnp.where((c == 2 * r) | (c == 2 * r + 1), 1.0, 0.0).astype(F32)


def pairs_lanes(in_lanes, out_lanes, shift=0):
    r = lax.broadcasted_iota(jnp.int32, (in_lanes, out_lanes), 0)
    c = lax.broadcasted_iota(jnp.int32, (in_lanes, out_lanes), 1) - shift
    return jnp.where((r == 2 * c) | (r == 2 * c + 1), 1.0, 0.0).astype(F32)


def dot(a, b):
    return jnp.dot(a, b, precision=lax.Precision.HIGHEST, preferred_element_type=F32)


def full_smooth(n, field, step, coefs, zero_start):
    if not zero_start:
        sweep(0, n, field, step, coefs, None, 1.0 / THETA)
    for keep, gain in chebyshev():
        sweep(0, n, field, step, coefs, keep, gain)


def coarse_cycle(levels, level):
    n, cond, right, field, step, coefs, temp, scale = levels[level]
    build(cond, n, right, coefs, field, step, scale)
    field[n] = jnp.zeros(field.shape[1:], F32)
    full_smooth(n, field, step, coefs, True)
    if level == len(levels) - 1:
        full_smooth(n, field, step, coefs, False)
        return
    half, below, below_right, below_field = n // 2, *levels[level + 1][1:4]
    rows, lanes = field.shape[1:]
    out_rows, out_lanes = below_field.shape[1:]

    def keep_resid(start, xs, results):
        for j, z in enumerate(results):
            temp[start + j] = z * coefs[2][start + j]

    residuals(0, n, field, coefs, keep_resid)
    merge = pairs_rows(half * out_rows, half * rows)
    squeeze = pairs_lanes(lanes, out_lanes)
    for source, target in ((temp, below_right), (cond, below)):
        both = source[...].reshape(half, 2, rows, lanes)
        both = (both[:, 0] + both[:, 1]).reshape(half * rows, lanes)
        target[...] = (dot(dot(merge, both), squeeze) * 0.125).reshape(half, out_rows, out_lanes)
    coarse_cycle(levels, level + 1)
    error = below_field[pl.ds(0, half)].reshape(half * out_rows, out_lanes)
    split = lax.broadcasted_iota(jnp.int32, (half * rows, half * out_rows), 0) // 2
    split = jnp.where(
        split == lax.broadcasted_iota(jnp.int32, (half * rows, half * out_rows), 1), 1.0, 0.0
    )
    spread = lax.broadcasted_iota(jnp.int32, (out_lanes, lanes), 1) // 2
    spread = jnp.where(
        spread == lax.broadcasted_iota(jnp.int32, (out_lanes, lanes), 0), 1.0, 0.0
    )
    error = dot(dot(split, error), spread).reshape(half, rows, lanes)
    for i in range(half):
        field[2 * i] = field[2 * i] + error[i]
        field[2 * i + 1] = field[2 * i + 1] + error[i]
    full_smooth(n, field, step, coefs, False)


def halo_kernel(sizes, heat, material, table, ext, pack, got, sems_out, sems_in):
    nx, ny, nz = sizes
    ix, iy, iz = lax.axis_index("gx"), lax.axis_index("gy"), lax.axis_index("gz")
    bx, by, bz = heat.shape
    ext[...] = jnp.zeros(ext.shape, F32)
    got[...] = jnp.zeros(got.shape, F32)
    own = (pl.ds(HX, bx), pl.ds(HY, by), pl.ds(0, bz))
    ext[(0, *own)] = heat[...]
    cond = jnp.zeros(heat.shape, F32)
    for which in range(MATERIALS):
        cond = cond + jnp.where(material[...] == which, table[which], 0.0)
    ext[(1, *own)] = cond

    sides = []
    for axis, at, count in (("gx", ix, nx), ("gy", iy, ny), ("gz", iz, nz)):
        sides.append((axis, at > 0, at - 1))
        sides.append((axis, at < count - 1, at + 1))

    barrier = pltpu.get_barrier_semaphore()
    for axis, there, other in sides:
        @pl.when(there)
        def _():
            pl.semaphore_signal(barrier, inc=1, device_id={axis: other}, device_id_type=MESH)
    pl.semaphore_wait(barrier, sum(jnp.where(there, 1, 0) for _, there, _ in sides))

    def exchange(which, low_source, low_target, high_source, high_target):
        copies = []
        for turn, (source, target) in enumerate(
            ((low_source, low_target), (high_source, high_target))
        ):
            axis, there, other = sides[which + turn]
            copy = pltpu.make_async_remote_copy(
                src_ref=source,
                dst_ref=target,
                send_sem=sems_out.at[which + turn],
                recv_sem=sems_in.at[which + turn],
                device_id={axis: other},
                device_id_type=MESH,
            )
            copies.append((there, copy))
            pl.when(there)(copy.start)
        pl.when(copies[0][0])(copies[1][1].wait_recv)
        pl.when(copies[1][0])(copies[0][1].wait_recv)
        pl.when(copies[0][0])(copies[0][1].wait_send)
        pl.when(copies[1][0])(copies[1][1].wait_send)

    def rows(start):
        return ext.at[:, pl.ds(HX, bx), pl.ds(start, HY), pl.ds(0, bz)]

    exchange(2, rows(HY), rows(HY + by), rows(by), rows(0))

    lane = lax.broadcasted_iota(jnp.int32, (ext.shape[2], bz), 1)
    for part in range(2):
        low = jnp.zeros((ext.shape[2], bz), F32)
        high = low
        for x in range(bx):
            v = ext[part, HX + x, :, pl.ds(0, bz)]
            mine = (lane >= HZ * x) & (lane < HZ * (x + 1))
            low = jnp.where(mine, pltpu.roll(v, (HZ * x) % bz, 1), low)
            high = jnp.where(mine, pltpu.roll(v, HZ * (x + 1) % bz, 1), high)
        pack[0, part] = low
        pack[1, part] = high
    exchange(4, pack.at[0], got.at[1], pack.at[1], got.at[0])
    for part in range(2):
        left, right = got[0, part], got[1, part]
        for x in range(bx):
            v = jnp.where(lane < HZ, pltpu.roll(right, (bz - HZ * x) % bz, 1), 0.0)
            v = jnp.where(lane >= bz - HZ, pltpu.roll(left, (2 * bz - HZ * (x + 1)) % bz, 1), v)
            ext[part, HX + x, :, pl.ds(bz, bz)] = v

    def planes(start):
        return ext.at[:, pl.ds(start, HX)]

    exchange(0, planes(HX), planes(HX + bx), planes(bx), planes(0))


def pre_kernel(ext, faces, over, field, packed, diagonal, step, temp):
    n = ext.shape[1]
    bx, by, bz = n - 2 * HX, ext.shape[2] - 2 * HY, ext.shape[3] // 2
    right, cond = ext.at[0], ext.at[1]
    coefs = (faces, over, diagonal)
    build(cond, n, right, coefs, field, step, 1.0, True)
    for keep, gain in chebyshev():
        sweep(2, n - 2, field, step, coefs, keep, gain)

    def keep_resid(start, xs, results):
        for j, z in enumerate(results):
            i = start + j
            temp[i - HX] = (z * diagonal[i])[HY:HY + by, :bz]

    residuals(HX, HX + bx, field, coefs, keep_resid)
    merge = pairs_rows(bx // 2 * by // 2, bx // 2 * by)
    result = jnp.zeros((bx // 2 * by // 2, bz), F32)
    for shift, source in (
        (0, temp[...]),
        (bz // 2, cond[pl.ds(HX, bx), pl.ds(HY, by), pl.ds(0, bz)]),
    ):
        both = source.reshape(bx // 2, 2, by, bz)
        both = (both[:, 0] + both[:, 1]).reshape(bx // 2 * by, bz)
        squeeze = pairs_lanes(bz, bz, shift)
        if shift == 0:
            lane = lax.broadcasted_iota(jnp.int32, (bz, bz), 1)
            squeeze = jnp.where(lane < bz // 2, squeeze, 0.0)
        result = result + dot(dot(merge, both), squeeze)
    packed[...] = (result * 0.125).reshape(bx // 2, by // 2, bz)


def gather_kernel(sizes, block, full, sems_out, sems_in):
    nx, ny, nz = sizes
    ix, iy, iz = lax.axis_index("gx"), lax.axis_index("gy"), lax.axis_index("gz")
    partners = []
    for axis, at, count in (("gy", iy, ny), ("gz", iz, nz), ("gx", ix, nx)):
        partners.append([(axis, lax.rem(at + off, count)) for off in range(1, count)])
    full[ix, iz, iy] = block[...]
    barrier = pltpu.get_barrier_semaphore()
    total = 0
    for group in partners:
        for axis, other in group:
            pl.semaphore_signal(barrier, inc=1, device_id={axis: other}, device_id_type=MESH)
            total += 1
    pl.semaphore_wait(barrier, total)
    slot = 0
    sent = []
    for group, source in zip(partners, (full.at[ix, iz, iy], full.at[ix, iz], full.at[ix])):
        copies = []
        for axis, other in group:
            copy = pltpu.make_async_remote_copy(
                src_ref=source,
                dst_ref=source,
                send_sem=sems_out.at[slot],
                recv_sem=sems_in.at[slot],
                device_id={axis: other},
                device_id_type=MESH,
            )
            copy.start()
            copies.append(copy)
            slot += 1
        for copy in copies:
            copy.wait_recv()
        sent += copies
    for copy in sent:
        copy.wait_send()


def post_kernel(sizes, faces, over, start, full, out, *scratch):
    nx, ny, nz = sizes
    ix, iy, iz = lax.axis_index("gx"), lax.axis_index("gy"), lax.axis_index("gz")
    n = start.shape[0]
    bx, by, bz = out.shape
    field, step = scratch[:2]
    levels, place, scale = [], 2, 0.25
    pad = HX // 2
    for level in range(1, LEVELS + 1):
        cond, right, whole, moves, temp, *coefs = scratch[place:place + 8]
        place += 8
        planes = cond.shape[0]
        values = whole.at[pl.ds(pad, planes + 1)] if level == 1 else whole
        if level == 1:
            coarse = whole
        levels.append((planes, cond, right, values, moves, tuple(coefs), temp, scale))
        scale *= 0.25
    _, cond, right = levels[0][:3]

    cx, cy = bx // 2, by // 2
    lane = lax.broadcasted_iota(jnp.int32, (cy, bz), 1)

    def assemble(i, _):
        for px in range(nx):
            for q in range(nz // 2):
                for py in range(ny):
                    one, two = full[px, 2 * q, py, i], full[px, 2 * q + 1, py, i]
                    where = (px * cx + i, pl.ds(py * cy, cy), pl.ds(q * bz, bz))
                    right[where] = jnp.where(lane < bz // 2, one, pltpu.roll(two, bz // 2, 1))
                    cond[where] = jnp.where(lane < bz // 2, pltpu.roll(one, bz // 2, 1), two)
        return 0

    lax.fori_loop(0, cx, assemble, 0)
    zero = jnp.zeros((pad, *coarse.shape[1:]), F32)
    coarse[pl.ds(0, pad)] = zero
    coarse[pl.ds(coarse.shape[0] - pad, pad)] = zero
    coarse_cycle(levels, 0)

    rows, lanes = start.shape[1:]
    crows, clanes = coarse.shape[1:]
    r = lax.broadcasted_iota(jnp.int32, (rows, crows), 0)
    c = lax.broadcasted_iota(jnp.int32, (rows, crows), 1)
    fine = 2 * (c - cy * iy) + HY
    split = jnp.where((r == fine) | (r == fine + 1), 1.0, 0.0).astype(F32)
    r = lax.broadcasted_iota(jnp.int32, (clanes, lanes), 0)
    c = lax.broadcasted_iota(jnp.int32, (clanes, lanes), 1)
    c = jnp.where(c >= lanes - HZ, c - lanes, c)
    fine = 2 * (r - bz // 2 * iz)
    spread = jnp.where((c == fine) | (c == fine + 1), 1.0, 0.0).astype(F32)

    window = coarse[pl.ds(cx * ix, n // 2)].reshape(n // 2 * crows, clanes)
    window = dot(window, spread).reshape(n // 2, crows, lanes)
    for i in range(n // 2):
        error = dot(split, window[i])
        field[2 * i] = start[2 * i] + error
        field[2 * i + 1] = start[2 * i + 1] + error
    coefs = (faces, over)
    low = HX - 2
    sweep(low, n - low, field, step, coefs, None, 1.0 / THETA)
    for turn, (keep, gain) in enumerate(chebyshev()):
        low = HX - 2 if turn == 0 else HX
        sweep(low, n - low, field, step, coefs, keep, gain)
    for i in range(bx):
        out[i] = field[HX + i, HY:HY + by, :bz]


def local(sizes, heat, material, table):
    nx, ny, nz = sizes
    bx, by, bz = heat.shape
    n, rows, lanes = bx + 2 * HX, by + 2 * HY, 2 * bz
    vmem = pl.BlockSpec(memory_space=pltpu.VMEM)
    smem = pl.BlockSpec(memory_space=pltpu.SMEM)
    limit = 30 * 1024 * 1024
    array = jax.ShapeDtypeStruct
    ext = pl.pallas_call(
        functools.partial(halo_kernel, sizes),
        out_shape=array((2, n, rows, lanes), F32),
        in_specs=[vmem, vmem, smem],
        out_specs=vmem,
        scratch_shapes=[
            pltpu.VMEM((2, 2, rows, bz), F32),
            pltpu.VMEM((2, 2, rows, bz), F32),
            pltpu.SemaphoreType.DMA((6,)),
            pltpu.SemaphoreType.DMA((6,)),
        ],
        compiler_params=pltpu.CompilerParams(
            collective_id=0, has_side_effects=True, vmem_limit_bytes=limit
        ),
    )(heat, material, table)
    fine = pltpu.VMEM((n, rows, lanes), F32)
    faces, over, start, packed = pl.pallas_call(
        pre_kernel,
        out_shape=[
            array((6, n, rows, lanes), F32),
            array((n, rows, lanes), F32),
            array((n, rows, lanes), F32),
            array((bx // 2, by // 2, bz), F32),
        ],
        in_specs=[vmem],
        out_specs=[vmem] * 4,
        scratch_shapes=[fine] * 2 + [pltpu.VMEM((bx, by, bz), F32)],
        compiler_params=pltpu.CompilerParams(vmem_limit_bytes=limit),
    )(ext)
    count = nx + ny + nz - 3
    full = pl.pallas_call(
        functools.partial(gather_kernel, sizes),
        out_shape=array((nx, nz, ny, bx // 2, by // 2, bz), F32),
        in_specs=[vmem],
        out_specs=vmem,
        scratch_shapes=[pltpu.SemaphoreType.DMA((count,)), pltpu.SemaphoreType.DMA((count,))],
        compiler_params=pltpu.CompilerParams(
            collective_id=1, has_side_effects=True, vmem_limit_bytes=limit
        ),
    )(packed)
    scratch = [fine] * 2
    for level in range(1, LEVELS + 1):
        shape = (bx * nx >> level, by * ny >> level, max(bz * nz >> level, 128))
        extra = HX if level == 1 else 1
        scratch += [pltpu.VMEM(shape, F32)] * 2
        scratch += [pltpu.VMEM((shape[0] + extra, *shape[1:]), F32)]
        scratch += [pltpu.VMEM(shape, F32)] * 2
        scratch += [pltpu.VMEM((6, *shape), F32)]
        scratch += [pltpu.VMEM(shape, F32)] * 2
    return pl.pallas_call(
        functools.partial(post_kernel, sizes),
        out_shape=array(heat.shape, F32),
        in_specs=[vmem] * 4,
        out_specs=vmem,
        scratch_shapes=scratch,
        compiler_params=pltpu.CompilerParams(vmem_limit_bytes=limit),
    )(faces, over, start, full)


def with_halo(block, sides):
    for axis, dim in sides:
        count = lax.axis_size(axis)
        forward = [(i, i + 1) for i in range(count - 1)]
        backward = [(target, source) for source, target in forward]
        low = lax.ppermute(
            lax.slice_in_dim(block, block.shape[dim] - 1, None, axis=dim), axis, forward
        )
        high = lax.ppermute(lax.slice_in_dim(block, 0, 1, axis=dim), axis, backward)
        block = jnp.concatenate([low, block, high], axis=dim)
    return block


def neighbours(block):
    padded = with_halo(block, (("gx", 0), ("gy", 1), ("gz", 2)))
    return (
        padded[2:, 1:-1, 1:-1],
        padded[:-2, 1:-1, 1:-1],
        padded[1:-1, 2:, 1:-1],
        padded[1:-1, :-2, 1:-1],
        padded[1:-1, 1:-1, 2:],
        padded[1:-1, 1:-1, :-2],
    )


def large_smooth(right, start, faces, diag, scale):
    inverse = 1.0 / (scale * diag)
    if start is None:
        step = inverse * right / THETA
        field = step
    else:
        step = inverse * large_resid(right, start, faces, diag, scale) / THETA
        field = start + step
    for keep, gain in chebyshev():
        step = keep * step + gain * inverse * large_resid(right, field, faces, diag, scale)
        field = field + step
    return field


def large_resid(right, field, faces, diag, scale):
    total = sum(face * near for face, near in zip(faces, neighbours(field)))
    return right - scale * (diag * field - total)


def restrict(field):
    sx, sy, sz = field.shape
    return field.reshape(sx // 2, 2, sy // 2, 2, sz // 2, 2).mean(axis=(1, 3, 5))


def large_cycle(right, cond, level, scale):
    faces = []
    for other in neighbours(cond):
        other = jnp.where(other > 0.0, other, cond)
        faces.append(2.0 * cond * other / (cond + other))
    diag = sum(faces)
    field = large_smooth(right, None, faces, diag, scale)
    if level < LEVELS:
        resid = large_resid(right, field, faces, diag, scale)
        error = large_cycle(restrict(resid), restrict(cond), level + 1, scale * 0.25)
        for dim in range(3):
            error = jnp.repeat(error, 2, dim)
        field = field + error
    return large_smooth(right, field, faces, diag, scale)


def large(heat, material, table):
    cond = jnp.zeros(heat.shape, F32)
    for which in range(MATERIALS):
        cond = cond + jnp.where(material == which, table[which], 0.0)
    return large_cycle(heat, cond, 0, 1.0)


def solution(mesh):
    sizes = tuple(mesh.shape[axis] for axis in ("gx", "gy", "gz"))

    def run(heat, material, table):
        small = heat.size // 8 <= 1 << 18
        body = functools.partial(local, sizes) if small else large
        spec = P("gx", "gy", "gz")
        return jax.shard_map(
            body, mesh=mesh, in_specs=(spec, spec, P()), out_specs=spec, check_vma=False
        )(heat, material, table)

    return run
```

```python
import functools

import jax
import jax.numpy as jnp
from jax import lax
from jax.experimental import pallas as pl
from jax.experimental.pallas import tpu as pltpu
from jax.sharding import PartitionSpec as P

DEGREE = 3
LEVELS = 3
MATERIALS = 3

LOW = 0.3
HIGH = 2.0
THETA = 0.5 * (HIGH + LOW)
DELTA = 0.5 * (HIGH - LOW)
SIGMA = THETA / DELTA

HX = 6
HY = 8
HZ = 8
MESH = pl.DeviceIdType.MESH
F32 = jnp.float32


def chebyshev():
    rho = 1.0 / SIGMA
    pairs = []
    for _ in range(DEGREE - 1):
        new = 1.0 / (2.0 * SIGMA - rho)
        pairs.append((new * rho, 2.0 * new / DELTA))
        rho = new
    return pairs


def up(v, axis):
    return pltpu.roll(v, v.shape[axis] - 1, axis)


def down(v, axis):
    return pltpu.roll(v, 1, axis)


def harmonic(a, b):
    return 2.0 * a * b / jnp.maximum(a + b, 1e-30)


def build(cond, n, right, coefs, field, step, scale, ring=False):
    faces, over, diagonal = coefs
    shape = cond.shape[1:]
    row = lax.broadcasted_iota(jnp.int32, shape, 0)
    lane = lax.broadcasted_iota(jnp.int32, shape, 1)

    def plane(i, k, k_low, k_high, fx_low):
        ky_high = jnp.where(row == shape[0] - 1, 0.0, up(k, 0))
        ky_low = jnp.where(row == 0, 0.0, down(k, 0))
        kz_high, kz_low = up(k, 1), down(k, 1)
        if not ring:
            kz_high = jnp.where(lane == shape[1] - 1, 0.0, kz_high)
            kz_low = jnp.where(lane == 0, 0.0, kz_low)
        fx, fy, fz = harmonic(k, k_high), harmonic(k, ky_high), harmonic(k, kz_high)
        missing = jnp.zeros(shape, F32)
        for other in (k_low, k_high, ky_low, ky_high, kz_low, kz_high):
            missing = missing + jnp.where(other > 0.0, 0.0, k)
        fy_low, fz_low = down(fy, 0), down(fz, 1)
        diag = fx + fx_low + fy + fy_low + fz + fz_low + missing
        inverse = jnp.where(k > 0.0, 1.0 / jnp.maximum(diag, 1e-30), 0.0)
        for side, face in enumerate((fx, fx_low, fy, fy_low, fz, fz_low)):
            faces[side, i] = face * inverse
        value = inverse * (1.0 / scale) * right[i]
        over[i] = value
        diagonal[i] = diag * scale
        field[i] = value * (1.0 / THETA)
        step[i] = value * (1.0 / THETA)
        return fx

    def body(i, carry):
        k, k_low, fx_low = carry
        k_high = cond[i + 1]
        fx = plane(i, k, k_low, k_high, fx_low)
        return k_high, k, fx

    zero = jnp.zeros(shape, F32)
    unroll = True if n <= 8 else 3
    k, k_low, fx_low = lax.fori_loop(0, n - 1, body, (cond[0], zero, zero), unroll=unroll)
    plane(n - 1, k, k_low, zero, fx_low)


def residuals(lo, hi, field, coefs, use):
    faces, over = coefs[:2]
    group = min(hi - lo, 8 if field.shape[1] <= 16 else 4)

    def body(turn, carry):
        start = lo + turn * group
        xs = list(carry) + [field[start + j + 1] for j in range(group)]
        results = []
        for j in range(group):
            i, x = start + j, xs[j + 1]
            along_x = faces[0, i] * xs[j + 2] + faces[1, i] * xs[j]
            along_y = faces[2, i] * up(x, 0) + faces[3, i] * down(x, 0)
            along_z = faces[4, i] * up(x, 1) + faces[5, i] * down(x, 1)
            results.append(((over[i] - x) + along_x) + (along_y + along_z))
        use(start, xs[1:-1], results)
        return xs[-2], xs[-1]

    low = field[lo - 1] if lo > 0 else jnp.zeros(field.shape[1:], F32)
    lax.fori_loop(0, (hi - lo) // group, body, (low, field[lo]))


def sweep(lo, hi, field, step, coefs, keep, gain):
    def use(start, xs, results):
        moves = [gain * z for z in results]
        if keep is not None:
            moves = [keep * step[start + j] + move for j, move in enumerate(moves)]
        for j, (x, move) in enumerate(zip(xs, moves)):
            step[start + j] = move
            field[start + j] = x + move

    residuals(lo, hi, field, coefs, use)


def pairs_rows(out_rows, in_rows):
    r = lax.broadcasted_iota(jnp.int32, (out_rows, in_rows), 0)
    c = lax.broadcasted_iota(jnp.int32, (out_rows, in_rows), 1)
    return jnp.where((c == 2 * r) | (c == 2 * r + 1), 1.0, 0.0).astype(F32)


def pairs_lanes(in_lanes, out_lanes, shift=0):
    r = lax.broadcasted_iota(jnp.int32, (in_lanes, out_lanes), 0)
    c = lax.broadcasted_iota(jnp.int32, (in_lanes, out_lanes), 1) - shift
    return jnp.where((r == 2 * c) | (r == 2 * c + 1), 1.0, 0.0).astype(F32)


def dot(a, b):
    return jnp.dot(a, b, precision=lax.Precision.HIGHEST, preferred_element_type=F32)


def full_smooth(n, field, step, coefs, zero_start):
    if not zero_start:
        sweep(0, n, field, step, coefs, None, 1.0 / THETA)
    for keep, gain in chebyshev():
        sweep(0, n, field, step, coefs, keep, gain)


def coarse_cycle(levels, level):
    n, cond, right, field, step, coefs, temp, scale = levels[level]
    build(cond, n, right, coefs, field, step, scale)
    field[n] = jnp.zeros(field.shape[1:], F32)
    full_smooth(n, field, step, coefs, True)
    if level == len(levels) - 1:
        full_smooth(n, field, step, coefs, False)
        return
    half, below, below_right, below_field = n // 2, *levels[level + 1][1:4]
    rows, lanes = field.shape[1:]
    out_rows, out_lanes = below_field.shape[1:]

    def keep_resid(start, xs, results):
        for j, z in enumerate(results):
            temp[start + j] = z * coefs[2][start + j]

    residuals(0, n, field, coefs, keep_resid)
    merge = pairs_rows(half * out_rows, half * rows)
    squeeze = pairs_lanes(lanes, out_lanes)
    for source, target in ((temp, below_right), (cond, below)):
        both = source[...].reshape(half, 2, rows, lanes)
        both = (both[:, 0] + both[:, 1]).reshape(half * rows, lanes)
        target[...] = (dot(dot(merge, both), squeeze) * 0.125).reshape(half, out_rows, out_lanes)
    coarse_cycle(levels, level + 1)
    error = below_field[pl.ds(0, half)].reshape(half * out_rows, out_lanes)
    split = lax.broadcasted_iota(jnp.int32, (half * rows, half * out_rows), 0) // 2
    split = jnp.where(
        split == lax.broadcasted_iota(jnp.int32, (half * rows, half * out_rows), 1), 1.0, 0.0
    )
    spread = lax.broadcasted_iota(jnp.int32, (out_lanes, lanes), 1) // 2
    spread = jnp.where(
        spread == lax.broadcasted_iota(jnp.int32, (out_lanes, lanes), 0), 1.0, 0.0
    )
    error = dot(dot(split, error), spread).reshape(half, rows, lanes)
    for i in range(half):
        field[2 * i] = field[2 * i] + error[i]
        field[2 * i + 1] = field[2 * i + 1] + error[i]
    full_smooth(n, field, step, coefs, False)


def pack_block(values):
    bx, by, bz = values.shape
    rows = bx // 2 * by // 2
    both = values.reshape(bx // 2, 2, by, bz)
    both = (both[:, 0] + both[:, 1]).reshape(bx // 2 * by, bz)
    both = dot(pairs_rows(rows, 2 * rows), both)
    low = dot(both[:rows // 2], pairs_lanes(bz, bz))
    high = dot(both[rows // 2:], pairs_lanes(bz, bz, bz // 2))
    return ((low + high) * 0.125).reshape(bx // 4, by // 2, bz)


def partner_groups(sizes, places):
    groups = []
    for which in (1, 2, 0):
        axis, at, count = ("gx", "gy", "gz")[which], places[which], sizes[which]
        groups.append([(axis, lax.rem(at + off, count)) for off in range(1, count)])
    return groups


def greet(groups):
    barrier = pltpu.get_barrier_semaphore()
    for group in groups:
        for axis, other in group:
            pl.semaphore_signal(barrier, inc=1, device_id={axis: other}, device_id_type=MESH)


def await_greetings(groups):
    pl.semaphore_wait(pltpu.get_barrier_semaphore(), sum(len(group) for group in groups))


def gather_stages(places, groups, full, sems_out, sems_in):
    ix, iy, iz = places
    slot = 0
    stages = []
    for group, source in zip(groups, (full.at[ix, iz, iy], full.at[ix, iz], full.at[ix])):
        stage = []
        for axis, other in group:
            stage.append(
                pltpu.make_async_remote_copy(
                    src_ref=source,
                    dst_ref=source,
                    send_sem=sems_out.at[slot],
                    recv_sem=sems_in.at[slot],
                    device_id={axis: other},
                    device_id_type=MESH,
                )
            )
            slot += 1
        stages.append(stage)
    return stages


def start_stage(stage):
    for copy in stage:
        copy.start()


def end_stage(stage):
    for copy in stage:
        copy.wait_recv()


def halo_kernel(
    sizes, heat, material, table, ext, full,
    heat_here, material_here, pack, got, sems_out, sems_in, gather_out, gather_in, sems_load,
):
    nx, ny, nz = sizes
    places = ix, iy, iz = tuple(lax.axis_index(axis) for axis in ("gx", "gy", "gz"))
    bx, by, bz = heat.shape
    loads = [
        pltpu.make_async_copy(heat, heat_here, sems_load.at[0]),
        pltpu.make_async_copy(material, material_here, sems_load.at[1]),
    ]
    for load in loads:
        load.start()
    ext[...] = jnp.zeros(ext.shape, F32)
    got[...] = jnp.zeros(got.shape, F32)
    groups = partner_groups(sizes, places)
    greet(groups)
    for load in loads:
        load.wait()
    own = (pl.ds(HX, bx), pl.ds(HY, by), pl.ds(0, bz))
    ext[(0, *own)] = heat_here[...]
    cond = jnp.zeros((bx, by, bz), F32)
    for which in range(MATERIALS):
        cond = cond + jnp.where(material_here[...] == which, table[which], 0.0)
    ext[(1, *own)] = cond
    lane = lax.broadcasted_iota(jnp.int32, (by, bz), 1)
    for part in range(2):
        low = jnp.zeros((by, bz), F32)
        high = low
        for x in range(bx):
            v = ext[part, HX + x, pl.ds(HY, by), pl.ds(0, bz)]
            mine = (lane >= HZ * x) & (lane < HZ * (x + 1))
            low = jnp.where(mine, pltpu.roll(v, (HZ * x) % bz, 1), low)
            high = jnp.where(mine, pltpu.roll(v, HZ * (x + 1) % bz, 1), high)
        pack[0, part] = low
        pack[1, part] = high

    sides = []
    for axis, at, count in (("gx", ix, nx), ("gy", iy, ny), ("gz", iz, nz)):
        sides.append((axis, at > 0, at - 1))
        sides.append((axis, at < count - 1, at + 1))

    def send(which, slot, low_source, low_target, high_source, high_target):
        copies = []
        for turn, (source, target) in enumerate(
            ((low_source, low_target), (high_source, high_target))
        ):
            axis, there, other = sides[which + turn]
            copy = pltpu.make_async_remote_copy(
                src_ref=source,
                dst_ref=target,
                send_sem=sems_out.at[slot + turn],
                recv_sem=sems_in.at[slot + turn],
                device_id={axis: other},
                device_id_type=MESH,
            )
            copies.append((there, copy))
            pl.when(there)(copy.start)
        return copies

    def receive(copies):
        pl.when(copies[0][0])(copies[1][1].wait_recv)
        pl.when(copies[1][0])(copies[0][1].wait_recv)

    def rows(start):
        return ext.at[:, pl.ds(HX, bx), pl.ds(start, HY), pl.ds(0, bz)]

    def planes(start):
        return ext.at[:, pl.ds(start, HX)]

    middle = pl.ds(HY, by)
    await_greetings(groups)
    sent = [
        send(4, 4, pack.at[0], got.at[1, :, middle], pack.at[1], got.at[0, :, middle]),
        send(2, 2, rows(HY), rows(HY + by), rows(by), rows(0)),
    ]
    full[ix, iz, iy] = pack_block(cond)
    stages = gather_stages(places, groups, full, gather_out, gather_in)
    start_stage(stages[0])
    receive(sent[0])

    def edges(start):
        return got.at[:, :, pl.ds(start, HY)]

    sent.append(send(2, 6, edges(HY), edges(HY + by), edges(by), edges(0)))
    receive(sent[2])
    lane = lax.broadcasted_iota(jnp.int32, (ext.shape[2], bz), 1)
    for part in range(2):
        left, right = got[0, part], got[1, part]
        for x in range(bx):
            v = jnp.where(lane < HZ, pltpu.roll(right, (bz - HZ * x) % bz, 1), 0.0)
            v = jnp.where(lane >= bz - HZ, pltpu.roll(left, (2 * bz - HZ * (x + 1)) % bz, 1), v)
            ext[part, HX + x, :, pl.ds(bz, bz)] = v
    end_stage(stages[0])
    start_stage(stages[1])
    receive(sent[1])
    sent.append(send(0, 0, planes(HX), planes(HX + bx), planes(bx), planes(0)))
    end_stage(stages[1])
    start_stage(stages[2])
    receive(sent[3])
    end_stage(stages[2])
    for copies in sent:
        for there, copy in copies:
            pl.when(there)(copy.wait_send)
    for stage in stages:
        for copy in stage:
            copy.wait_send()


def pre_kernel(ext, faces, over, field, packed, diagonal, step, temp):
    n = ext.shape[1]
    bx, by, bz = n - 2 * HX, ext.shape[2] - 2 * HY, ext.shape[3] // 2
    right, cond = ext.at[0], ext.at[1]
    coefs = (faces, over, diagonal)
    build(cond, n, right, coefs, field, step, 1.0, True)
    for keep, gain in chebyshev():
        sweep(2, n - 2, field, step, coefs, keep, gain)

    def keep_resid(start, xs, results):
        for j, z in enumerate(results):
            i = start + j
            temp[i - HX] = (z * diagonal[i])[HY:HY + by, :bz]

    residuals(HX, HX + bx, field, coefs, keep_resid)
    packed[...] = pack_block(temp[...])


def gather_kernel(sizes, block, full, sems_out, sems_in):
    places = ix, iy, iz = tuple(lax.axis_index(axis) for axis in ("gx", "gy", "gz"))
    groups = partner_groups(sizes, places)
    greet(groups)
    full[ix, iz, iy] = block[...]
    await_greetings(groups)
    stages = gather_stages(places, groups, full, sems_out, sems_in)
    for stage in stages:
        start_stage(stage)
        end_stage(stage)
    for stage in stages:
        for copy in stage:
            copy.wait_send()


def post_kernel(sizes, faces, over, start, full_right, full_cond, out, *scratch):
    nx, ny, nz = sizes
    ix, iy, iz = lax.axis_index("gx"), lax.axis_index("gy"), lax.axis_index("gz")
    n = start.shape[0]
    bx, by, bz = out.shape
    field, step = scratch[:2]
    levels, place, scale = [], 2, 0.25
    pad = HX // 2
    for level in range(1, LEVELS + 1):
        cond, right, whole, moves, temp, *coefs = scratch[place:place + 8]
        place += 8
        planes = cond.shape[0]
        values = whole.at[pl.ds(pad, planes + 1)] if level == 1 else whole
        if level == 1:
            coarse = whole
        levels.append((planes, cond, right, values, moves, tuple(coefs), temp, scale))
        scale *= 0.25
    _, cond, right = levels[0][:3]

    cx, cy = bx // 2, by // 2
    lane = lax.broadcasted_iota(jnp.int32, (cy, bz), 1)

    for full, target in ((full_right, right), (full_cond, cond)):
        for px in range(nx):
            for q in range(nz // 2):
                for py in range(ny):
                    for i in range(cx // 2):
                        one, two = full[px, 2 * q, py, i], full[px, 2 * q + 1, py, i]
                        place = (pl.ds(py * cy, cy), pl.ds(q * bz, bz))
                        low = jnp.where(lane < bz // 2, one, pltpu.roll(two, bz // 2, 1))
                        high = jnp.where(lane < bz // 2, pltpu.roll(one, bz // 2, 1), two)
                        target[(px * cx + i, *place)] = low
                        target[(px * cx + cx // 2 + i, *place)] = high
    zero = jnp.zeros((pad, *coarse.shape[1:]), F32)
    coarse[pl.ds(0, pad)] = zero
    coarse[pl.ds(coarse.shape[0] - pad, pad)] = zero
    coarse_cycle(levels, 0)

    rows, lanes = start.shape[1:]
    crows, clanes = coarse.shape[1:]
    r = lax.broadcasted_iota(jnp.int32, (rows, crows), 0)
    c = lax.broadcasted_iota(jnp.int32, (rows, crows), 1)
    fine = 2 * (c - cy * iy) + HY
    split = jnp.where((r == fine) | (r == fine + 1), 1.0, 0.0).astype(F32)
    r = lax.broadcasted_iota(jnp.int32, (clanes, lanes), 0)
    c = lax.broadcasted_iota(jnp.int32, (clanes, lanes), 1)
    c = jnp.where(c >= lanes - HZ, c - lanes, c)
    fine = 2 * (r - bz // 2 * iz)
    spread = jnp.where((c == fine) | (c == fine + 1), 1.0, 0.0).astype(F32)

    window = coarse[pl.ds(cx * ix, n // 2)].reshape(n // 2 * crows, clanes)
    window = dot(window, spread).reshape(n // 2, crows, lanes)
    for i in range(n // 2):
        error = dot(split, window[i])
        field[2 * i] = start[2 * i] + error
        field[2 * i + 1] = start[2 * i + 1] + error
    coefs = (faces, over)
    low = HX - 2
    sweep(low, n - low, field, step, coefs, None, 1.0 / THETA)
    for turn, (keep, gain) in enumerate(chebyshev()):
        low = HX - 2 if turn == 0 else HX
        sweep(low, n - low, field, step, coefs, keep, gain)
    for i in range(bx):
        out[i] = field[HX + i, HY:HY + by, :bz]


def local(sizes, heat, material, table):
    nx, ny, nz = sizes
    bx, by, bz = heat.shape
    n, rows, lanes = bx + 2 * HX, by + 2 * HY, 2 * bz
    vmem = pl.BlockSpec(memory_space=pltpu.VMEM)
    smem = pl.BlockSpec(memory_space=pltpu.SMEM)
    limit = 30 * 1024 * 1024
    array = jax.ShapeDtypeStruct
    hbm = pl.BlockSpec(memory_space=pltpu.HBM)
    count = nx + ny + nz - 3
    coarse = array((nx, nz, ny, bx // 4, by // 2, bz), F32)
    dma = pltpu.SemaphoreType.DMA
    ext, full_cond = pl.pallas_call(
        functools.partial(halo_kernel, sizes),
        out_shape=[array((2, n, rows, lanes), F32), coarse],
        in_specs=[hbm, hbm, smem],
        out_specs=[vmem, vmem],
        scratch_shapes=[
            pltpu.VMEM(heat.shape, F32),
            pltpu.VMEM(heat.shape, jnp.int32),
            pltpu.VMEM((2, 2, by, bz), F32),
            pltpu.VMEM((2, 2, rows, bz), F32),
            dma((8,)),
            dma((8,)),
            dma((count,)),
            dma((count,)),
            dma((2,)),
        ],
        compiler_params=pltpu.CompilerParams(
            collective_id=0, has_side_effects=True, vmem_limit_bytes=limit
        ),
    )(heat, material, table)
    fine = pltpu.VMEM((n, rows, lanes), F32)
    faces, over, start, packed = pl.pallas_call(
        pre_kernel,
        out_shape=[
            array((6, n, rows, lanes), F32),
            array((n, rows, lanes), F32),
            array((n, rows, lanes), F32),
            array((bx // 4, by // 2, bz), F32),
        ],
        in_specs=[vmem],
        out_specs=[vmem] * 4,
        scratch_shapes=[fine] * 2 + [pltpu.VMEM((bx, by, bz), F32)],
        compiler_params=pltpu.CompilerParams(vmem_limit_bytes=limit),
    )(ext)
    full_right = pl.pallas_call(
        functools.partial(gather_kernel, sizes),
        out_shape=coarse,
        in_specs=[vmem],
        out_specs=vmem,
        scratch_shapes=[pltpu.SemaphoreType.DMA((count,)), pltpu.SemaphoreType.DMA((count,))],
        compiler_params=pltpu.CompilerParams(
            collective_id=1, has_side_effects=True, vmem_limit_bytes=limit
        ),
    )(packed)
    scratch = [fine] * 2
    for level in range(1, LEVELS + 1):
        shape = (bx * nx >> level, by * ny >> level, max(bz * nz >> level, 128))
        extra = HX if level == 1 else 1
        scratch += [pltpu.VMEM(shape, F32)] * 2
        scratch += [pltpu.VMEM((shape[0] + extra, *shape[1:]), F32)]
        scratch += [pltpu.VMEM(shape, F32)] * 2
        scratch += [pltpu.VMEM((6, *shape), F32)]
        scratch += [pltpu.VMEM(shape, F32)] * 2
    return pl.pallas_call(
        functools.partial(post_kernel, sizes),
        out_shape=array(heat.shape, F32),
        in_specs=[vmem] * 5,
        out_specs=vmem,
        scratch_shapes=scratch,
        compiler_params=pltpu.CompilerParams(vmem_limit_bytes=limit),
    )(faces, over, start, full_right, full_cond)


def with_halo(block, sides):
    for axis, dim in sides:
        count = lax.axis_size(axis)
        forward = [(i, i + 1) for i in range(count - 1)]
        backward = [(target, source) for source, target in forward]
        low = lax.ppermute(
            lax.slice_in_dim(block, block.shape[dim] - 1, None, axis=dim), axis, forward
        )
        high = lax.ppermute(lax.slice_in_dim(block, 0, 1, axis=dim), axis, backward)
        block = jnp.concatenate([low, block, high], axis=dim)
    return block


def neighbours(block):
    padded = with_halo(block, (("gx", 0), ("gy", 1), ("gz", 2)))
    return (
        padded[2:, 1:-1, 1:-1],
        padded[:-2, 1:-1, 1:-1],
        padded[1:-1, 2:, 1:-1],
        padded[1:-1, :-2, 1:-1],
        padded[1:-1, 1:-1, 2:],
        padded[1:-1, 1:-1, :-2],
    )


def large_smooth(right, start, faces, diag, scale):
    inverse = 1.0 / (scale * diag)
    if start is None:
        step = inverse * right / THETA
        field = step
    else:
        step = inverse * large_resid(right, start, faces, diag, scale) / THETA
        field = start + step
    for keep, gain in chebyshev():
        step = keep * step + gain * inverse * large_resid(right, field, faces, diag, scale)
        field = field + step
    return field


def large_resid(right, field, faces, diag, scale):
    total = sum(face * near for face, near in zip(faces, neighbours(field)))
    return right - scale * (diag * field - total)


def restrict(field):
    sx, sy, sz = field.shape
    return field.reshape(sx // 2, 2, sy // 2, 2, sz // 2, 2).mean(axis=(1, 3, 5))


def large_cycle(right, cond, level, scale):
    faces = []
    for other in neighbours(cond):
        other = jnp.where(other > 0.0, other, cond)
        faces.append(2.0 * cond * other / (cond + other))
    diag = sum(faces)
    field = large_smooth(right, None, faces, diag, scale)
    if level < LEVELS:
        resid = large_resid(right, field, faces, diag, scale)
        error = large_cycle(restrict(resid), restrict(cond), level + 1, scale * 0.25)
        for dim in range(3):
            error = jnp.repeat(error, 2, dim)
        field = field + error
    return large_smooth(right, field, faces, diag, scale)


def large(heat, material, table):
    cond = jnp.zeros(heat.shape, F32)
    for which in range(MATERIALS):
        cond = cond + jnp.where(material == which, table[which], 0.0)
    return large_cycle(heat, cond, 0, 1.0)


def solution(mesh):
    sizes = tuple(mesh.shape[axis] for axis in ("gx", "gy", "gz"))

    def run(heat, material, table):
        small = heat.size // 8 <= 1 << 18
        body = functools.partial(local, sizes) if small else large
        spec = P("gx", "gy", "gz")
        return jax.shard_map(
            body, mesh=mesh, in_specs=(spec, spec, P()), out_specs=spec, check_vma=False
        )(heat, material, table)

    return run
```

```python
import functools

import jax
import jax.numpy as jnp
from jax import lax
from jax.experimental import pallas as pl
from jax.experimental.pallas import tpu as pltpu
from jax.sharding import PartitionSpec as P

DEGREE = 3
LEVELS = 3
MATERIALS = 3

LOW = 0.3
HIGH = 2.0
THETA = 0.5 * (HIGH + LOW)
DELTA = 0.5 * (HIGH - LOW)
SIGMA = THETA / DELTA

HX = 6
HY = 8
HZ = 8
MESH = pl.DeviceIdType.MESH
F32 = jnp.float32


def chebyshev():
    rho = 1.0 / SIGMA
    pairs = []
    for _ in range(DEGREE - 1):
        new = 1.0 / (2.0 * SIGMA - rho)
        pairs.append((new * rho, 2.0 * new / DELTA))
        rho = new
    return pairs


def up(v, axis):
    return pltpu.roll(v, v.shape[axis] - 1, axis)


def down(v, axis):
    return pltpu.roll(v, 1, axis)


def harmonic(a, b):
    return 2.0 * a * b / jnp.maximum(a + b, 1e-30)


def build(cond, n, right, coefs, field, step, scale, ring=False):
    faces, over, diagonal = coefs
    shape = cond.shape[1:]
    row = lax.broadcasted_iota(jnp.int32, shape, 0)
    lane = lax.broadcasted_iota(jnp.int32, shape, 1)

    def plane(i, k, k_low, k_high, fx_low):
        ky_high = jnp.where(row == shape[0] - 1, 0.0, up(k, 0))
        ky_low = jnp.where(row == 0, 0.0, down(k, 0))
        kz_high, kz_low = up(k, 1), down(k, 1)
        if not ring:
            kz_high = jnp.where(lane == shape[1] - 1, 0.0, kz_high)
            kz_low = jnp.where(lane == 0, 0.0, kz_low)
        fx, fy, fz = harmonic(k, k_high), harmonic(k, ky_high), harmonic(k, kz_high)
        missing = jnp.zeros(shape, F32)
        for other in (k_low, k_high, ky_low, ky_high, kz_low, kz_high):
            missing = missing + jnp.where(other > 0.0, 0.0, k)
        fy_low, fz_low = down(fy, 0), down(fz, 1)
        diag = fx + fx_low + fy + fy_low + fz + fz_low + missing
        inverse = jnp.where(k > 0.0, 1.0 / jnp.maximum(diag, 1e-30), 0.0)
        for side, face in enumerate((fx, fx_low, fy, fy_low, fz, fz_low)):
            faces[side, i] = face * inverse
        value = inverse * (1.0 / scale) * right[i]
        over[i] = value
        diagonal[i] = diag * scale
        field[i] = value * (1.0 / THETA)
        step[i] = value * (1.0 / THETA)
        return fx

    def body(i, carry):
        k, k_low, fx_low = carry
        k_high = cond[i + 1]
        fx = plane(i, k, k_low, k_high, fx_low)
        return k_high, k, fx

    zero = jnp.zeros(shape, F32)
    unroll = True if n <= 8 else 3
    k, k_low, fx_low = lax.fori_loop(0, n - 1, body, (cond[0], zero, zero), unroll=unroll)
    plane(n - 1, k, k_low, zero, fx_low)


def residuals(lo, hi, field, coefs, use):
    faces, over = coefs[:2]
    group = min(hi - lo, 8 if field.shape[1] <= 16 else 4)

    def body(turn, carry):
        start = lo + turn * group
        xs = list(carry) + [field[start + j + 1] for j in range(group)]
        results = []
        for j in range(group):
            i, x = start + j, xs[j + 1]
            along_x = faces[0, i] * xs[j + 2] + faces[1, i] * xs[j]
            along_y = faces[2, i] * up(x, 0) + faces[3, i] * down(x, 0)
            along_z = faces[4, i] * up(x, 1) + faces[5, i] * down(x, 1)
            results.append(((over[i] - x) + along_x) + (along_y + along_z))
        use(start, xs[1:-1], results)
        return xs[-2], xs[-1]

    low = field[lo - 1] if lo > 0 else jnp.zeros(field.shape[1:], F32)
    lax.fori_loop(0, (hi - lo) // group, body, (low, field[lo]))


def sweep(lo, hi, field, step, coefs, keep, gain):
    def use(start, xs, results):
        moves = [gain * z for z in results]
        if keep is not None:
            moves = [keep * step[start + j] + move for j, move in enumerate(moves)]
        for j, (x, move) in enumerate(zip(xs, moves)):
            step[start + j] = move
            field[start + j] = x + move

    residuals(lo, hi, field, coefs, use)


def pairs_rows(out_rows, in_rows):
    r = lax.broadcasted_iota(jnp.int32, (out_rows, in_rows), 0)
    c = lax.broadcasted_iota(jnp.int32, (out_rows, in_rows), 1)
    return jnp.where((c == 2 * r) | (c == 2 * r + 1), 1.0, 0.0).astype(F32)


def pairs_lanes(in_lanes, out_lanes, shift=0):
    r = lax.broadcasted_iota(jnp.int32, (in_lanes, out_lanes), 0)
    c = lax.broadcasted_iota(jnp.int32, (in_lanes, out_lanes), 1) - shift
    return jnp.where((r == 2 * c) | (r == 2 * c + 1), 1.0, 0.0).astype(F32)


def dot(a, b):
    return jnp.dot(a, b, precision=lax.Precision.HIGHEST, preferred_element_type=F32)


def full_smooth(n, field, step, coefs, zero_start):
    if not zero_start:
        sweep(0, n, field, step, coefs, None, 1.0 / THETA)
    for keep, gain in chebyshev():
        sweep(0, n, field, step, coefs, keep, gain)


def coarse_cycle(levels, level):
    n, cond, right, field, step, coefs, temp, scale = levels[level]
    build(cond, n, right, coefs, field, step, scale)
    field[n] = jnp.zeros(field.shape[1:], F32)
    full_smooth(n, field, step, coefs, True)
    if level == len(levels) - 1:
        full_smooth(n, field, step, coefs, False)
        return
    half, below, below_right, below_field = n // 2, *levels[level + 1][1:4]
    rows, lanes = field.shape[1:]
    out_rows, out_lanes = below_field.shape[1:]

    def keep_resid(start, xs, results):
        for j, z in enumerate(results):
            temp[start + j] = z * coefs[2][start + j]

    residuals(0, n, field, coefs, keep_resid)
    merge = pairs_rows(half * out_rows, half * rows)
    squeeze = pairs_lanes(lanes, out_lanes)
    for source, target in ((temp, below_right), (cond, below)):
        both = source[...].reshape(half, 2, rows, lanes)
        both = (both[:, 0] + both[:, 1]).reshape(half * rows, lanes)
        target[...] = (dot(dot(merge, both), squeeze) * 0.125).reshape(half, out_rows, out_lanes)
    coarse_cycle(levels, level + 1)
    error = below_field[pl.ds(0, half)].reshape(half * out_rows, out_lanes)
    split = lax.broadcasted_iota(jnp.int32, (half * rows, half * out_rows), 0) // 2
    split = jnp.where(
        split == lax.broadcasted_iota(jnp.int32, (half * rows, half * out_rows), 1), 1.0, 0.0
    )
    spread = lax.broadcasted_iota(jnp.int32, (out_lanes, lanes), 1) // 2
    spread = jnp.where(
        spread == lax.broadcasted_iota(jnp.int32, (out_lanes, lanes), 0), 1.0, 0.0
    )
    error = dot(dot(split, error), spread).reshape(half, rows, lanes)
    for i in range(half):
        field[2 * i] = field[2 * i] + error[i]
        field[2 * i + 1] = field[2 * i + 1] + error[i]
    full_smooth(n, field, step, coefs, False)


def pack_block(values):
    bx, by, bz = values.shape
    rows = bx // 2 * by // 2
    both = values.reshape(bx // 2, 2, by, bz)
    both = (both[:, 0] + both[:, 1]).reshape(bx // 2 * by, bz)
    both = dot(pairs_rows(rows, 2 * rows), both)
    low = dot(both[:rows // 2], pairs_lanes(bz, bz))
    high = dot(both[rows // 2:], pairs_lanes(bz, bz, bz // 2))
    return ((low + high) * 0.125).reshape(bx // 4, by // 2, bz)


def partner_groups(sizes, places):
    groups = []
    for which in (1, 2, 0):
        axis, at, count = ("gx", "gy", "gz")[which], places[which], sizes[which]
        groups.append([(axis, lax.rem(at + off, count)) for off in range(1, count)])
    return groups


def greet(groups):
    barrier = pltpu.get_barrier_semaphore()
    for group in groups:
        for axis, other in group:
            pl.semaphore_signal(barrier, inc=1, device_id={axis: other}, device_id_type=MESH)


def await_greetings(groups):
    pl.semaphore_wait(pltpu.get_barrier_semaphore(), sum(len(group) for group in groups))


def gather_stages(places, groups, full, sems_out, sems_in):
    ix, iy, iz = places
    slot = 0
    stages = []
    for group, source in zip(groups, (full.at[ix, iz, iy], full.at[ix, iz], full.at[ix])):
        stage = []
        for axis, other in group:
            stage.append(
                pltpu.make_async_remote_copy(
                    src_ref=source,
                    dst_ref=source,
                    send_sem=sems_out.at[slot],
                    recv_sem=sems_in.at[slot],
                    device_id={axis: other},
                    device_id_type=MESH,
                )
            )
            slot += 1
        stages.append(stage)
    return stages


def start_stage(stage):
    for copy in stage:
        copy.start()


def end_stage(stage):
    for copy in stage:
        copy.wait_recv()


def halo_kernel(
    sizes, inputs, ext, full, pack, got, sems_out, sems_in, gather_out, gather_in
):
    nx, ny, nz = sizes
    places = ix, iy, iz = tuple(lax.axis_index(axis) for axis in ("gx", "gy", "gz"))
    bx, by, bz = inputs.shape[1:]
    ext[...] = jnp.zeros(ext.shape, F32)
    got[...] = jnp.zeros(got.shape, F32)
    groups = partner_groups(sizes, places)
    greet(groups)
    ext[:, pl.ds(HX, bx), pl.ds(HY, by), pl.ds(0, bz)] = inputs[...]
    lane = lax.broadcasted_iota(jnp.int32, (by, bz), 1)
    for part in range(2):
        low = jnp.zeros((by, bz), F32)
        high = low
        for x in range(bx):
            v = ext[part, HX + x, pl.ds(HY, by), pl.ds(0, bz)]
            mine = (lane >= HZ * x) & (lane < HZ * (x + 1))
            low = jnp.where(mine, pltpu.roll(v, (HZ * x) % bz, 1), low)
            high = jnp.where(mine, pltpu.roll(v, HZ * (x + 1) % bz, 1), high)
        pack[0, part] = low
        pack[1, part] = high

    sides = []
    for axis, at, count in (("gx", ix, nx), ("gy", iy, ny), ("gz", iz, nz)):
        sides.append((axis, at > 0, at - 1))
        sides.append((axis, at < count - 1, at + 1))

    def send(which, slot, low_source, low_target, high_source, high_target):
        copies = []
        for turn, (source, target) in enumerate(
            ((low_source, low_target), (high_source, high_target))
        ):
            axis, there, other = sides[which + turn]
            copy = pltpu.make_async_remote_copy(
                src_ref=source,
                dst_ref=target,
                send_sem=sems_out.at[slot + turn],
                recv_sem=sems_in.at[slot + turn],
                device_id={axis: other},
                device_id_type=MESH,
            )
            copies.append((there, copy))
            pl.when(there)(copy.start)
        return copies

    def receive(copies):
        pl.when(copies[0][0])(copies[1][1].wait_recv)
        pl.when(copies[1][0])(copies[0][1].wait_recv)

    def rows(start):
        return ext.at[:, pl.ds(HX, bx), pl.ds(start, HY), pl.ds(0, bz)]

    def planes(start):
        return ext.at[:, pl.ds(start, HX)]

    middle = pl.ds(HY, by)
    full[ix, iz, iy] = pack_block(inputs[1])
    stages = gather_stages(places, groups, full, gather_out, gather_in)
    await_greetings(groups)
    start_stage(stages[0])
    sent = [
        send(4, 4, pack.at[0], got.at[1, :, middle], pack.at[1], got.at[0, :, middle]),
        send(2, 2, rows(HY), rows(HY + by), rows(by), rows(0)),
    ]
    receive(sent[0])

    def edges(start):
        return got.at[:, :, pl.ds(start, HY)]

    sent.append(send(2, 6, edges(HY), edges(HY + by), edges(by), edges(0)))
    end_stage(stages[0])
    start_stage(stages[1])
    receive(sent[2])
    lane = lax.broadcasted_iota(jnp.int32, (ext.shape[2], bz), 1)
    for part in range(2):
        left, right = got[0, part], got[1, part]
        for x in range(bx):
            v = jnp.where(lane < HZ, pltpu.roll(right, (bz - HZ * x) % bz, 1), 0.0)
            v = jnp.where(lane >= bz - HZ, pltpu.roll(left, (2 * bz - HZ * (x + 1)) % bz, 1), v)
            ext[part, HX + x, :, pl.ds(bz, bz)] = v
    receive(sent[1])
    sent.append(send(0, 0, planes(HX), planes(HX + bx), planes(bx), planes(0)))
    end_stage(stages[1])
    start_stage(stages[2])
    receive(sent[3])
    end_stage(stages[2])
    for copies in sent:
        for there, copy in copies:
            pl.when(there)(copy.wait_send)
    for stage in stages:
        for copy in stage:
            copy.wait_send()


def pre_kernel(ext, faces, over, field, packed, diagonal, step, temp):
    n = ext.shape[1]
    bx, by, bz = n - 2 * HX, ext.shape[2] - 2 * HY, ext.shape[3] // 2
    right, cond = ext.at[0], ext.at[1]
    coefs = (faces, over, diagonal)
    build(cond, n, right, coefs, field, step, 1.0, True)
    for keep, gain in chebyshev():
        sweep(2, n - 2, field, step, coefs, keep, gain)

    def keep_resid(start, xs, results):
        for j, z in enumerate(results):
            i = start + j
            temp[i - HX] = (z * diagonal[i])[HY:HY + by, :bz]

    residuals(HX, HX + bx, field, coefs, keep_resid)
    packed[...] = pack_block(temp[...])


def gather_kernel(sizes, block, full, sems_out, sems_in):
    places = ix, iy, iz = tuple(lax.axis_index(axis) for axis in ("gx", "gy", "gz"))
    groups = partner_groups(sizes, places)
    greet(groups)
    full[ix, iz, iy] = block[...]
    await_greetings(groups)
    stages = gather_stages(places, groups, full, sems_out, sems_in)
    for stage in stages:
        start_stage(stage)
        end_stage(stage)
    for stage in stages:
        for copy in stage:
            copy.wait_send()


def post_kernel(sizes, faces, over, start, full_right, full_cond, out, *scratch):
    nx, ny, nz = sizes
    ix, iy, iz = lax.axis_index("gx"), lax.axis_index("gy"), lax.axis_index("gz")
    n = start.shape[0]
    bx, by, bz = out.shape
    field, step = scratch[:2]
    levels, place, scale = [], 2, 0.25
    pad = HX // 2
    for level in range(1, LEVELS + 1):
        cond, right, whole, moves, temp, *coefs = scratch[place:place + 8]
        place += 8
        planes = cond.shape[0]
        values = whole.at[pl.ds(pad, planes + 1)] if level == 1 else whole
        if level == 1:
            coarse = whole
        levels.append((planes, cond, right, values, moves, tuple(coefs), temp, scale))
        scale *= 0.25
    _, cond, right = levels[0][:3]

    cx, cy = bx // 2, by // 2
    lane = lax.broadcasted_iota(jnp.int32, (cy, bz), 1)

    for full, target in ((full_right, right), (full_cond, cond)):
        for px in range(nx):
            for q in range(nz // 2):
                for py in range(ny):
                    for i in range(cx // 2):
                        one, two = full[px, 2 * q, py, i], full[px, 2 * q + 1, py, i]
                        place = (pl.ds(py * cy, cy), pl.ds(q * bz, bz))
                        low = jnp.where(lane < bz // 2, one, pltpu.roll(two, bz // 2, 1))
                        high = jnp.where(lane < bz // 2, pltpu.roll(one, bz // 2, 1), two)
                        target[(px * cx + i, *place)] = low
                        target[(px * cx + cx // 2 + i, *place)] = high
    zero = jnp.zeros((pad, *coarse.shape[1:]), F32)
    coarse[pl.ds(0, pad)] = zero
    coarse[pl.ds(coarse.shape[0] - pad, pad)] = zero
    coarse_cycle(levels, 0)

    rows, lanes = start.shape[1:]
    crows, clanes = coarse.shape[1:]
    r = lax.broadcasted_iota(jnp.int32, (rows, crows), 0)
    c = lax.broadcasted_iota(jnp.int32, (rows, crows), 1)
    fine = 2 * (c - cy * iy) + HY
    split = jnp.where((r == fine) | (r == fine + 1), 1.0, 0.0).astype(F32)
    r = lax.broadcasted_iota(jnp.int32, (clanes, lanes), 0)
    c = lax.broadcasted_iota(jnp.int32, (clanes, lanes), 1)
    c = jnp.where(c >= lanes - HZ, c - lanes, c)
    fine = 2 * (r - bz // 2 * iz)
    spread = jnp.where((c == fine) | (c == fine + 1), 1.0, 0.0).astype(F32)

    window = coarse[pl.ds(cx * ix, n // 2)].reshape(n // 2 * crows, clanes)
    window = dot(window, spread).reshape(n // 2, crows, lanes)
    for i in range(n // 2):
        error = dot(split, window[i])
        field[2 * i] = start[2 * i] + error
        field[2 * i + 1] = start[2 * i + 1] + error
    coefs = (faces, over)
    low = HX - 2
    sweep(low, n - low, field, step, coefs, None, 1.0 / THETA)
    for turn, (keep, gain) in enumerate(chebyshev()):
        low = HX - 2 if turn == 0 else HX
        sweep(low, n - low, field, step, coefs, keep, gain)
    for i in range(bx):
        out[i] = field[HX + i, HY:HY + by, :bz]


def local(sizes, heat, material, table):
    nx, ny, nz = sizes
    bx, by, bz = heat.shape
    n, rows, lanes = bx + 2 * HX, by + 2 * HY, 2 * bz
    vmem = pl.BlockSpec(memory_space=pltpu.VMEM)
    limit = 30 * 1024 * 1024
    array = jax.ShapeDtypeStruct
    cond = jnp.zeros(heat.shape, F32)
    for which in range(MATERIALS):
        cond = cond + jnp.where(material == which, table[which], 0.0)
    count = nx + ny + nz - 3
    coarse = array((nx, nz, ny, bx // 4, by // 2, bz), F32)
    dma = pltpu.SemaphoreType.DMA
    ext, full_cond = pl.pallas_call(
        functools.partial(halo_kernel, sizes),
        out_shape=[array((2, n, rows, lanes), F32), coarse],
        in_specs=[vmem],
        out_specs=[vmem, vmem],
        scratch_shapes=[
            pltpu.VMEM((2, 2, by, bz), F32),
            pltpu.VMEM((2, 2, rows, bz), F32),
            dma((8,)),
            dma((8,)),
            dma((count,)),
            dma((count,)),
        ],
        compiler_params=pltpu.CompilerParams(
            collective_id=0, has_side_effects=True, vmem_limit_bytes=limit
        ),
    )(jnp.stack([heat, cond]))
    fine = pltpu.VMEM((n, rows, lanes), F32)
    faces, over, start, packed = pl.pallas_call(
        pre_kernel,
        out_shape=[
            array((6, n, rows, lanes), F32),
            array((n, rows, lanes), F32),
            array((n, rows, lanes), F32),
            array((bx // 4, by // 2, bz), F32),
        ],
        in_specs=[vmem],
        out_specs=[vmem] * 4,
        scratch_shapes=[fine] * 2 + [pltpu.VMEM((bx, by, bz), F32)],
        compiler_params=pltpu.CompilerParams(vmem_limit_bytes=limit),
    )(ext)
    full_right = pl.pallas_call(
        functools.partial(gather_kernel, sizes),
        out_shape=coarse,
        in_specs=[vmem],
        out_specs=vmem,
        scratch_shapes=[pltpu.SemaphoreType.DMA((count,)), pltpu.SemaphoreType.DMA((count,))],
        compiler_params=pltpu.CompilerParams(
            collective_id=1, has_side_effects=True, vmem_limit_bytes=limit
        ),
    )(packed)
    scratch = [fine] * 2
    for level in range(1, LEVELS + 1):
        shape = (bx * nx >> level, by * ny >> level, max(bz * nz >> level, 128))
        extra = HX if level == 1 else 1
        scratch += [pltpu.VMEM(shape, F32)] * 2
        scratch += [pltpu.VMEM((shape[0] + extra, *shape[1:]), F32)]
        scratch += [pltpu.VMEM(shape, F32)] * 2
        scratch += [pltpu.VMEM((6, *shape), F32)]
        scratch += [pltpu.VMEM(shape, F32)] * 2
    return pl.pallas_call(
        functools.partial(post_kernel, sizes),
        out_shape=array(heat.shape, F32),
        in_specs=[vmem] * 5,
        out_specs=vmem,
        scratch_shapes=scratch,
        compiler_params=pltpu.CompilerParams(vmem_limit_bytes=limit),
    )(faces, over, start, full_right, full_cond)


def with_halo(block, sides):
    for axis, dim in sides:
        count = lax.axis_size(axis)
        forward = [(i, i + 1) for i in range(count - 1)]
        backward = [(target, source) for source, target in forward]
        low = lax.ppermute(
            lax.slice_in_dim(block, block.shape[dim] - 1, None, axis=dim), axis, forward
        )
        high = lax.ppermute(lax.slice_in_dim(block, 0, 1, axis=dim), axis, backward)
        block = jnp.concatenate([low, block, high], axis=dim)
    return block


def neighbours(block):
    padded = with_halo(block, (("gx", 0), ("gy", 1), ("gz", 2)))
    return (
        padded[2:, 1:-1, 1:-1],
        padded[:-2, 1:-1, 1:-1],
        padded[1:-1, 2:, 1:-1],
        padded[1:-1, :-2, 1:-1],
        padded[1:-1, 1:-1, 2:],
        padded[1:-1, 1:-1, :-2],
    )


def large_smooth(right, start, faces, diag, scale):
    inverse = 1.0 / (scale * diag)
    if start is None:
        step = inverse * right / THETA
        field = step
    else:
        step = inverse * large_resid(right, start, faces, diag, scale) / THETA
        field = start + step
    for keep, gain in chebyshev():
        step = keep * step + gain * inverse * large_resid(right, field, faces, diag, scale)
        field = field + step
    return field


def large_resid(right, field, faces, diag, scale):
    total = sum(face * near for face, near in zip(faces, neighbours(field)))
    return right - scale * (diag * field - total)


def restrict(field):
    sx, sy, sz = field.shape
    return field.reshape(sx // 2, 2, sy // 2, 2, sz // 2, 2).mean(axis=(1, 3, 5))


def large_cycle(right, cond, level, scale):
    faces = []
    for other in neighbours(cond):
        other = jnp.where(other > 0.0, other, cond)
        faces.append(2.0 * cond * other / (cond + other))
    diag = sum(faces)
    field = large_smooth(right, None, faces, diag, scale)
    if level < LEVELS:
        resid = large_resid(right, field, faces, diag, scale)
        error = large_cycle(restrict(resid), restrict(cond), level + 1, scale * 0.25)
        for dim in range(3):
            error = jnp.repeat(error, 2, dim)
        field = field + error
    return large_smooth(right, field, faces, diag, scale)


def large(heat, material, table):
    cond = jnp.zeros(heat.shape, F32)
    for which in range(MATERIALS):
        cond = cond + jnp.where(material == which, table[which], 0.0)
    return large_cycle(heat, cond, 0, 1.0)


def solution(mesh):
    sizes = tuple(mesh.shape[axis] for axis in ("gx", "gy", "gz"))

    def run(heat, material, table):
        small = heat.size // 8 <= 1 << 18
        body = functools.partial(local, sizes) if small else large
        spec = P("gx", "gy", "gz")
        return jax.shard_map(
            body, mesh=mesh, in_specs=(spec, spec, P()), out_specs=spec, check_vma=False
        )(heat, material, table)

    return run
```

```python
import functools

import jax
import jax.numpy as jnp
from jax import lax
from jax.experimental import pallas as pl
from jax.experimental.pallas import tpu as pltpu
from jax.sharding import PartitionSpec as P

DEGREE = 3
LEVELS = 3
MATERIALS = 3

LOW = 0.3
HIGH = 2.0
THETA = 0.5 * (HIGH + LOW)
DELTA = 0.5 * (HIGH - LOW)
SIGMA = THETA / DELTA

HX = 6
HY = 8
HZ = 8
MESH = pl.DeviceIdType.MESH
F32 = jnp.float32


def chebyshev():
    rho = 1.0 / SIGMA
    pairs = []
    for _ in range(DEGREE - 1):
        new = 1.0 / (2.0 * SIGMA - rho)
        pairs.append((new * rho, 2.0 * new / DELTA))
        rho = new
    return pairs


def up(v, axis):
    return pltpu.roll(v, v.shape[axis] - 1, axis)


def down(v, axis):
    return pltpu.roll(v, 1, axis)


def harmonic(a, b):
    return 2.0 * a * b / jnp.maximum(a + b, 1e-30)


def build(cond, n, right, coefs, field, step, scale, ring=False):
    faces, over, diagonal = coefs
    shape = cond.shape[1:]
    row = lax.broadcasted_iota(jnp.int32, shape, 0)
    lane = lax.broadcasted_iota(jnp.int32, shape, 1)

    def plane(i, k, k_low, k_high, fx_low):
        ky_high = jnp.where(row == shape[0] - 1, 0.0, up(k, 0))
        ky_low = jnp.where(row == 0, 0.0, down(k, 0))
        kz_high, kz_low = up(k, 1), down(k, 1)
        if not ring:
            kz_high = jnp.where(lane == shape[1] - 1, 0.0, kz_high)
            kz_low = jnp.where(lane == 0, 0.0, kz_low)
        fx, fy, fz = harmonic(k, k_high), harmonic(k, ky_high), harmonic(k, kz_high)
        missing = jnp.zeros(shape, F32)
        for other in (k_low, k_high, ky_low, ky_high, kz_low, kz_high):
            missing = missing + jnp.where(other > 0.0, 0.0, k)
        fy_low, fz_low = down(fy, 0), down(fz, 1)
        diag = fx + fx_low + fy + fy_low + fz + fz_low + missing
        inverse = jnp.where(k > 0.0, 1.0 / jnp.maximum(diag, 1e-30), 0.0)
        for side, face in enumerate((fx, fx_low, fy, fy_low, fz, fz_low)):
            faces[side, i] = face * inverse
        value = inverse * (1.0 / scale) * right[i]
        over[i] = value
        diagonal[i] = diag * scale
        field[i] = value * (1.0 / THETA)
        step[i] = value * (1.0 / THETA)
        return fx

    def body(i, carry):
        k, k_low, fx_low = carry
        k_high = cond[i + 1]
        fx = plane(i, k, k_low, k_high, fx_low)
        return k_high, k, fx

    zero = jnp.zeros(shape, F32)
    unroll = True if n <= 8 else 3
    k, k_low, fx_low = lax.fori_loop(0, n - 1, body, (cond[0], zero, zero), unroll=unroll)
    plane(n - 1, k, k_low, zero, fx_low)


def residuals(lo, hi, field, coefs, use):
    faces, over = coefs[:2]
    group = min(hi - lo, 8 if field.shape[1] <= 16 else 4)

    def body(turn, carry):
        start = lo + turn * group
        xs = list(carry) + [field[start + j + 1] for j in range(group)]
        results = []
        for j in range(group):
            i, x = start + j, xs[j + 1]
            along_x = faces[0, i] * xs[j + 2] + faces[1, i] * xs[j]
            along_y = faces[2, i] * up(x, 0) + faces[3, i] * down(x, 0)
            along_z = faces[4, i] * up(x, 1) + faces[5, i] * down(x, 1)
            results.append(((over[i] - x) + along_x) + (along_y + along_z))
        use(start, xs[1:-1], results)
        return xs[-2], xs[-1]

    low = field[lo - 1] if lo > 0 else jnp.zeros(field.shape[1:], F32)
    lax.fori_loop(0, (hi - lo) // group, body, (low, field[lo]))


def sweep(lo, hi, field, step, coefs, keep, gain):
    def use(start, xs, results):
        moves = [gain * z for z in results]
        if keep is not None:
            moves = [keep * step[start + j] + move for j, move in enumerate(moves)]
        for j, (x, move) in enumerate(zip(xs, moves)):
            step[start + j] = move
            field[start + j] = x + move

    residuals(lo, hi, field, coefs, use)


def pairs_rows(out_rows, in_rows):
    r = lax.broadcasted_iota(jnp.int32, (out_rows, in_rows), 0)
    c = lax.broadcasted_iota(jnp.int32, (out_rows, in_rows), 1)
    return jnp.where((c == 2 * r) | (c == 2 * r + 1), 1.0, 0.0).astype(F32)


def pairs_lanes(in_lanes, out_lanes, shift=0):
    r = lax.broadcasted_iota(jnp.int32, (in_lanes, out_lanes), 0)
    c = lax.broadcasted_iota(jnp.int32, (in_lanes, out_lanes), 1) - shift
    return jnp.where((r == 2 * c) | (r == 2 * c + 1), 1.0, 0.0).astype(F32)


def dot(a, b):
    return jnp.dot(a, b, precision=lax.Precision.HIGHEST, preferred_element_type=F32)


def full_smooth(n, field, step, coefs, zero_start):
    if not zero_start:
        sweep(0, n, field, step, coefs, None, 1.0 / THETA)
    for keep, gain in chebyshev():
        sweep(0, n, field, step, coefs, keep, gain)


def coarse_cycle(levels, level):
    n, cond, right, field, step, coefs, temp, scale = levels[level]
    build(cond, n, right, coefs, field, step, scale)
    field[n] = jnp.zeros(field.shape[1:], F32)
    full_smooth(n, field, step, coefs, True)
    if level == len(levels) - 1:
        full_smooth(n, field, step, coefs, False)
        return
    half, below, below_right, below_field = n // 2, *levels[level + 1][1:4]
    rows, lanes = field.shape[1:]
    out_rows, out_lanes = below_field.shape[1:]

    def keep_resid(start, xs, results):
        for j, z in enumerate(results):
            temp[start + j] = z * coefs[2][start + j]

    residuals(0, n, field, coefs, keep_resid)
    merge = pairs_rows(half * out_rows, half * rows)
    squeeze = pairs_lanes(lanes, out_lanes)
    for source, target in ((temp, below_right), (cond, below)):
        both = source[...].reshape(half, 2, rows, lanes)
        both = (both[:, 0] + both[:, 1]).reshape(half * rows, lanes)
        target[...] = (dot(dot(merge, both), squeeze) * 0.125).reshape(half, out_rows, out_lanes)
    coarse_cycle(levels, level + 1)
    error = below_field[pl.ds(0, half)].reshape(half * out_rows, out_lanes)
    split = lax.broadcasted_iota(jnp.int32, (half * rows, half * out_rows), 0) // 2
    split = jnp.where(
        split == lax.broadcasted_iota(jnp.int32, (half * rows, half * out_rows), 1), 1.0, 0.0
    )
    spread = lax.broadcasted_iota(jnp.int32, (out_lanes, lanes), 1) // 2
    spread = jnp.where(
        spread == lax.broadcasted_iota(jnp.int32, (out_lanes, lanes), 0), 1.0, 0.0
    )
    error = dot(dot(split, error), spread).reshape(half, rows, lanes)
    for i in range(half):
        field[2 * i] = field[2 * i] + error[i]
        field[2 * i + 1] = field[2 * i + 1] + error[i]
    full_smooth(n, field, step, coefs, False)


def pack_block(values):
    bx, by, bz = values.shape
    rows = bx // 2 * by // 2
    both = values.reshape(bx // 2, 2, by, bz)
    both = (both[:, 0] + both[:, 1]).reshape(bx // 2 * by, bz)
    both = dot(pairs_rows(rows, 2 * rows), both)
    low = dot(both[:rows // 2], pairs_lanes(bz, bz))
    high = dot(both[rows // 2:], pairs_lanes(bz, bz, bz // 2))
    return ((low + high) * 0.125).reshape(bx // 4, by // 2, bz)


def partner_groups(sizes, places):
    groups = []
    for which in (1, 2, 0):
        axis, at, count = ("gx", "gy", "gz")[which], places[which], sizes[which]
        groups.append([(axis, lax.rem(at + off, count)) for off in range(1, count)])
    return groups


def greet(groups):
    barrier = pltpu.get_barrier_semaphore()
    for group in groups:
        for axis, other in group:
            pl.semaphore_signal(barrier, inc=1, device_id={axis: other}, device_id_type=MESH)


def await_greetings(groups):
    pl.semaphore_wait(pltpu.get_barrier_semaphore(), sum(len(group) for group in groups))


def gather_stages(places, groups, full, sems_out, sems_in):
    ix, iy, iz = places
    slot = 0
    stages = []
    for group, source in zip(groups, (full.at[ix, iz, iy], full.at[ix, iz], full.at[ix])):
        stage = []
        for axis, other in group:
            stage.append(
                pltpu.make_async_remote_copy(
                    src_ref=source,
                    dst_ref=source,
                    send_sem=sems_out.at[slot],
                    recv_sem=sems_in.at[slot],
                    device_id={axis: other},
                    device_id_type=MESH,
                )
            )
            slot += 1
        stages.append(stage)
    return stages


def start_stage(stage):
    for copy in stage:
        copy.start()


def end_stage(stage):
    for copy in stage:
        copy.wait_recv()


def halo_kernel(
    sizes, heat, material, table, ext, full,
    pack, got, sems_out, sems_in, gather_out, gather_in,
):
    nx, ny, nz = sizes
    places = ix, iy, iz = tuple(lax.axis_index(axis) for axis in ("gx", "gy", "gz"))
    bx, by, bz = heat.shape
    ext[...] = jnp.zeros(ext.shape, F32)
    got[...] = jnp.zeros(got.shape, F32)
    groups = partner_groups(sizes, places)
    greet(groups)
    own = (pl.ds(HX, bx), pl.ds(HY, by), pl.ds(0, bz))
    ext[(0, *own)] = heat[...]
    cond = jnp.zeros((bx, by, bz), F32)
    for which in range(MATERIALS):
        cond = cond + jnp.where(material[...] == which, table[which], 0.0)
    ext[(1, *own)] = cond
    lane = lax.broadcasted_iota(jnp.int32, (by, bz), 1)
    for part in range(2):
        low = jnp.zeros((by, bz), F32)
        high = low
        for x in range(bx):
            v = ext[part, HX + x, pl.ds(HY, by), pl.ds(0, bz)]
            mine = (lane >= HZ * x) & (lane < HZ * (x + 1))
            low = jnp.where(mine, pltpu.roll(v, (HZ * x) % bz, 1), low)
            high = jnp.where(mine, pltpu.roll(v, HZ * (x + 1) % bz, 1), high)
        pack[0, part] = low
        pack[1, part] = high

    sides = []
    for axis, at, count in (("gx", ix, nx), ("gy", iy, ny), ("gz", iz, nz)):
        sides.append((axis, at > 0, at - 1))
        sides.append((axis, at < count - 1, at + 1))

    def send(which, slot, low_source, low_target, high_source, high_target):
        copies = []
        for turn, (source, target) in enumerate(
            ((low_source, low_target), (high_source, high_target))
        ):
            axis, there, other = sides[which + turn]
            copy = pltpu.make_async_remote_copy(
                src_ref=source,
                dst_ref=target,
                send_sem=sems_out.at[slot + turn],
                recv_sem=sems_in.at[slot + turn],
                device_id={axis: other},
                device_id_type=MESH,
            )
            copies.append((there, copy))
            pl.when(there)(copy.start)
        return copies

    def receive(copies):
        pl.when(copies[0][0])(copies[1][1].wait_recv)
        pl.when(copies[1][0])(copies[0][1].wait_recv)

    def rows(start):
        return ext.at[:, pl.ds(HX, bx), pl.ds(start, HY), pl.ds(0, bz)]

    def planes(start):
        return ext.at[:, pl.ds(start, HX)]

    middle = pl.ds(HY, by)
    full[ix, iz, iy] = pack_block(cond)
    stages = gather_stages(places, groups, full, gather_out, gather_in)
    await_greetings(groups)
    start_stage(stages[0])
    sent = [
        send(4, 4, pack.at[0], got.at[1, :, middle], pack.at[1], got.at[0, :, middle]),
        send(2, 2, rows(HY), rows(HY + by), rows(by), rows(0)),
    ]
    receive(sent[0])

    def edges(start):
        return got.at[:, :, pl.ds(start, HY)]

    sent.append(send(2, 6, edges(HY), edges(HY + by), edges(by), edges(0)))
    end_stage(stages[0])
    start_stage(stages[1])
    receive(sent[2])
    lane = lax.broadcasted_iota(jnp.int32, (ext.shape[2], bz), 1)
    for part in range(2):
        left, right = got[0, part], got[1, part]
        for x in range(bx):
            v = jnp.where(lane < HZ, pltpu.roll(right, (bz - HZ * x) % bz, 1), 0.0)
            v = jnp.where(lane >= bz - HZ, pltpu.roll(left, (2 * bz - HZ * (x + 1)) % bz, 1), v)
            ext[part, HX + x, :, pl.ds(bz, bz)] = v
    receive(sent[1])
    sent.append(send(0, 0, planes(HX), planes(HX + bx), planes(bx), planes(0)))
    end_stage(stages[1])
    start_stage(stages[2])
    receive(sent[3])
    end_stage(stages[2])
    for copies in sent:
        for there, copy in copies:
            pl.when(there)(copy.wait_send)
    for stage in stages:
        for copy in stage:
            copy.wait_send()


def pre_kernel(ext, faces, over, field, packed, diagonal, step, temp):
    n = ext.shape[1]
    bx, by, bz = n - 2 * HX, ext.shape[2] - 2 * HY, ext.shape[3] // 2
    right, cond = ext.at[0], ext.at[1]
    coefs = (faces, over, diagonal)
    build(cond, n, right, coefs, field, step, 1.0, True)
    for keep, gain in chebyshev():
        sweep(2, n - 2, field, step, coefs, keep, gain)

    def keep_resid(start, xs, results):
        for j, z in enumerate(results):
            i = start + j
            temp[i - HX] = (z * diagonal[i])[HY:HY + by, :bz]

    residuals(HX, HX + bx, field, coefs, keep_resid)
    packed[...] = pack_block(temp[...])


def gather_kernel(sizes, block, full, sems_out, sems_in):
    places = ix, iy, iz = tuple(lax.axis_index(axis) for axis in ("gx", "gy", "gz"))
    groups = partner_groups(sizes, places)
    greet(groups)
    full[ix, iz, iy] = block[...]
    await_greetings(groups)
    stages = gather_stages(places, groups, full, sems_out, sems_in)
    for stage in stages:
        start_stage(stage)
        end_stage(stage)
    for stage in stages:
        for copy in stage:
            copy.wait_send()


def post_kernel(sizes, faces, over, start, full_right, full_cond, out, *scratch):
    nx, ny, nz = sizes
    ix, iy, iz = lax.axis_index("gx"), lax.axis_index("gy"), lax.axis_index("gz")
    n = start.shape[0]
    bx, by, bz = out.shape
    field, step = scratch[:2]
    levels, place, scale = [], 2, 0.25
    pad = HX // 2
    for level in range(1, LEVELS + 1):
        cond, right, whole, moves, temp, *coefs = scratch[place:place + 8]
        place += 8
        planes = cond.shape[0]
        values = whole.at[pl.ds(pad, planes + 1)] if level == 1 else whole
        if level == 1:
            coarse = whole
        levels.append((planes, cond, right, values, moves, tuple(coefs), temp, scale))
        scale *= 0.25
    _, cond, right = levels[0][:3]

    cx, cy = bx // 2, by // 2
    lane = lax.broadcasted_iota(jnp.int32, (cy, bz), 1)

    for full, target in ((full_right, right), (full_cond, cond)):
        for px in range(nx):
            for q in range(nz // 2):
                for py in range(ny):
                    for i in range(cx // 2):
                        one, two = full[px, 2 * q, py, i], full[px, 2 * q + 1, py, i]
                        place = (pl.ds(py * cy, cy), pl.ds(q * bz, bz))
                        low = jnp.where(lane < bz // 2, one, pltpu.roll(two, bz // 2, 1))
                        high = jnp.where(lane < bz // 2, pltpu.roll(one, bz // 2, 1), two)
                        target[(px * cx + i, *place)] = low
                        target[(px * cx + cx // 2 + i, *place)] = high
    zero = jnp.zeros((pad, *coarse.shape[1:]), F32)
    coarse[pl.ds(0, pad)] = zero
    coarse[pl.ds(coarse.shape[0] - pad, pad)] = zero
    coarse_cycle(levels, 0)

    rows, lanes = start.shape[1:]
    crows, clanes = coarse.shape[1:]
    r = lax.broadcasted_iota(jnp.int32, (rows, crows), 0)
    c = lax.broadcasted_iota(jnp.int32, (rows, crows), 1)
    fine = 2 * (c - cy * iy) + HY
    split = jnp.where((r == fine) | (r == fine + 1), 1.0, 0.0).astype(F32)
    r = lax.broadcasted_iota(jnp.int32, (clanes, lanes), 0)
    c = lax.broadcasted_iota(jnp.int32, (clanes, lanes), 1)
    c = jnp.where(c >= lanes - HZ, c - lanes, c)
    fine = 2 * (r - bz // 2 * iz)
    spread = jnp.where((c == fine) | (c == fine + 1), 1.0, 0.0).astype(F32)

    window = coarse[pl.ds(cx * ix, n // 2)].reshape(n // 2 * crows, clanes)
    window = dot(window, spread).reshape(n // 2, crows, lanes)
    for i in range(n // 2):
        error = dot(split, window[i])
        field[2 * i] = start[2 * i] + error
        field[2 * i + 1] = start[2 * i + 1] + error
    coefs = (faces, over)
    low = HX - 2
    sweep(low, n - low, field, step, coefs, None, 1.0 / THETA)
    for turn, (keep, gain) in enumerate(chebyshev()):
        low = HX - 2 if turn == 0 else HX
        sweep(low, n - low, field, step, coefs, keep, gain)
    for i in range(bx):
        out[i] = field[HX + i, HY:HY + by, :bz]


def local(sizes, heat, material, table):
    nx, ny, nz = sizes
    bx, by, bz = heat.shape
    n, rows, lanes = bx + 2 * HX, by + 2 * HY, 2 * bz
    vmem = pl.BlockSpec(memory_space=pltpu.VMEM)
    smem = pl.BlockSpec(memory_space=pltpu.SMEM)
    limit = 30 * 1024 * 1024
    array = jax.ShapeDtypeStruct
    count = nx + ny + nz - 3
    coarse = array((nx, nz, ny, bx // 4, by // 2, bz), F32)
    dma = pltpu.SemaphoreType.DMA
    ext, full_cond = pl.pallas_call(
        functools.partial(halo_kernel, sizes),
        out_shape=[array((2, n, rows, lanes), F32), coarse],
        in_specs=[vmem, vmem, smem],
        out_specs=[vmem, vmem],
        scratch_shapes=[
            pltpu.VMEM((2, 2, by, bz), F32),
            pltpu.VMEM((2, 2, rows, bz), F32),
            dma((8,)),
            dma((8,)),
            dma((count,)),
            dma((count,)),
        ],
        compiler_params=pltpu.CompilerParams(
            collective_id=0, has_side_effects=True, vmem_limit_bytes=limit
        ),
    )(heat, material, table)
    fine = pltpu.VMEM((n, rows, lanes), F32)
    faces, over, start, packed = pl.pallas_call(
        pre_kernel,
        out_shape=[
            array((6, n, rows, lanes), F32),
            array((n, rows, lanes), F32),
            array((n, rows, lanes), F32),
            array((bx // 4, by // 2, bz), F32),
        ],
        in_specs=[vmem],
        out_specs=[vmem] * 4,
        scratch_shapes=[fine] * 2 + [pltpu.VMEM((bx, by, bz), F32)],
        compiler_params=pltpu.CompilerParams(vmem_limit_bytes=limit),
    )(ext)
    full_right = pl.pallas_call(
        functools.partial(gather_kernel, sizes),
        out_shape=coarse,
        in_specs=[vmem],
        out_specs=vmem,
        scratch_shapes=[pltpu.SemaphoreType.DMA((count,)), pltpu.SemaphoreType.DMA((count,))],
        compiler_params=pltpu.CompilerParams(
            collective_id=1, has_side_effects=True, vmem_limit_bytes=limit
        ),
    )(packed)
    scratch = [fine] * 2
    for level in range(1, LEVELS + 1):
        shape = (bx * nx >> level, by * ny >> level, max(bz * nz >> level, 128))
        extra = HX if level == 1 else 1
        scratch += [pltpu.VMEM(shape, F32)] * 2
        scratch += [pltpu.VMEM((shape[0] + extra, *shape[1:]), F32)]
        scratch += [pltpu.VMEM(shape, F32)] * 2
        scratch += [pltpu.VMEM((6, *shape), F32)]
        scratch += [pltpu.VMEM(shape, F32)] * 2
    return pl.pallas_call(
        functools.partial(post_kernel, sizes),
        out_shape=array(heat.shape, F32),
        in_specs=[vmem] * 5,
        out_specs=vmem,
        scratch_shapes=scratch,
        compiler_params=pltpu.CompilerParams(vmem_limit_bytes=limit),
    )(faces, over, start, full_right, full_cond)


def with_halo(block, sides):
    for axis, dim in sides:
        count = lax.axis_size(axis)
        forward = [(i, i + 1) for i in range(count - 1)]
        backward = [(target, source) for source, target in forward]
        low = lax.ppermute(
            lax.slice_in_dim(block, block.shape[dim] - 1, None, axis=dim), axis, forward
        )
        high = lax.ppermute(lax.slice_in_dim(block, 0, 1, axis=dim), axis, backward)
        block = jnp.concatenate([low, block, high], axis=dim)
    return block


def neighbours(block):
    padded = with_halo(block, (("gx", 0), ("gy", 1), ("gz", 2)))
    return (
        padded[2:, 1:-1, 1:-1],
        padded[:-2, 1:-1, 1:-1],
        padded[1:-1, 2:, 1:-1],
        padded[1:-1, :-2, 1:-1],
        padded[1:-1, 1:-1, 2:],
        padded[1:-1, 1:-1, :-2],
    )


def large_smooth(right, start, faces, diag, scale):
    inverse = 1.0 / (scale * diag)
    if start is None:
        step = inverse * right / THETA
        field = step
    else:
        step = inverse * large_resid(right, start, faces, diag, scale) / THETA
        field = start + step
    for keep, gain in chebyshev():
        step = keep * step + gain * inverse * large_resid(right, field, faces, diag, scale)
        field = field + step
    return field


def large_resid(right, field, faces, diag, scale):
    total = sum(face * near for face, near in zip(faces, neighbours(field)))
    return right - scale * (diag * field - total)


def restrict(field):
    sx, sy, sz = field.shape
    return field.reshape(sx // 2, 2, sy // 2, 2, sz // 2, 2).mean(axis=(1, 3, 5))


def large_cycle(right, cond, level, scale):
    faces = []
    for other in neighbours(cond):
        other = jnp.where(other > 0.0, other, cond)
        faces.append(2.0 * cond * other / (cond + other))
    diag = sum(faces)
    field = large_smooth(right, None, faces, diag, scale)
    if level < LEVELS:
        resid = large_resid(right, field, faces, diag, scale)
        error = large_cycle(restrict(resid), restrict(cond), level + 1, scale * 0.25)
        for dim in range(3):
            error = jnp.repeat(error, 2, dim)
        field = field + error
    return large_smooth(right, field, faces, diag, scale)


def large(heat, material, table):
    cond = jnp.zeros(heat.shape, F32)
    for which in range(MATERIALS):
        cond = cond + jnp.where(material == which, table[which], 0.0)
    return large_cycle(heat, cond, 0, 1.0)


def solution(mesh):
    sizes = tuple(mesh.shape[axis] for axis in ("gx", "gy", "gz"))

    def run(heat, material, table):
        small = heat.size // 8 <= 1 << 18
        body = functools.partial(local, sizes) if small else large
        spec = P("gx", "gy", "gz")
        return jax.shard_map(
            body, mesh=mesh, in_specs=(spec, spec, P()), out_specs=spec, check_vma=False
        )(heat, material, table)

    return run
```

```python
import functools

import jax
import jax.numpy as jnp
from jax import lax
from jax.experimental import pallas as pl
from jax.experimental.pallas import tpu as pltpu
from jax.sharding import PartitionSpec as P

DEGREE = 3
LEVELS = 3
MATERIALS = 3

LOW = 0.3
HIGH = 2.0
THETA = 0.5 * (HIGH + LOW)
DELTA = 0.5 * (HIGH - LOW)
SIGMA = THETA / DELTA

HX = 6
HY = 8
HZ = 8
MESH = pl.DeviceIdType.MESH
F32 = jnp.float32


def chebyshev():
    rho = 1.0 / SIGMA
    pairs = []
    for _ in range(DEGREE - 1):
        new = 1.0 / (2.0 * SIGMA - rho)
        pairs.append((new * rho, 2.0 * new / DELTA))
        rho = new
    return pairs


def up(v, axis):
    return pltpu.roll(v, v.shape[axis] - 1, axis)


def down(v, axis):
    return pltpu.roll(v, 1, axis)


def harmonic(a, b):
    return 2.0 * a * b / jnp.maximum(a + b, 1e-30)


def build(cond, n, right, coefs, field, step, scale, ring=False):
    faces, over, diagonal = coefs
    shape = cond.shape[1:]
    row = lax.broadcasted_iota(jnp.int32, shape, 0)
    lane = lax.broadcasted_iota(jnp.int32, shape, 1)

    def plane(i, k, k_low, k_high, fx_low):
        ky_high = jnp.where(row == shape[0] - 1, 0.0, up(k, 0))
        ky_low = jnp.where(row == 0, 0.0, down(k, 0))
        kz_high, kz_low = up(k, 1), down(k, 1)
        if not ring:
            kz_high = jnp.where(lane == shape[1] - 1, 0.0, kz_high)
            kz_low = jnp.where(lane == 0, 0.0, kz_low)
        fx, fy, fz = harmonic(k, k_high), harmonic(k, ky_high), harmonic(k, kz_high)
        missing = jnp.zeros(shape, F32)
        for other in (k_low, k_high, ky_low, ky_high, kz_low, kz_high):
            missing = missing + jnp.where(other > 0.0, 0.0, k)
        fy_low, fz_low = down(fy, 0), down(fz, 1)
        diag = fx + fx_low + fy + fy_low + fz + fz_low + missing
        inverse = jnp.where(k > 0.0, 1.0 / jnp.maximum(diag, 1e-30), 0.0)
        for side, face in enumerate((fx, fx_low, fy, fy_low, fz, fz_low)):
            faces[side, i] = face * inverse
        value = inverse * (1.0 / scale) * right[i]
        over[i] = value
        diagonal[i] = diag * scale
        field[i] = value * (1.0 / THETA)
        step[i] = value * (1.0 / THETA)
        return fx

    def body(i, carry):
        k, k_low, fx_low = carry
        k_high = cond[i + 1]
        fx = plane(i, k, k_low, k_high, fx_low)
        return k_high, k, fx

    zero = jnp.zeros(shape, F32)
    unroll = True if n <= 8 else 3
    k, k_low, fx_low = lax.fori_loop(0, n - 1, body, (cond[0], zero, zero), unroll=unroll)
    plane(n - 1, k, k_low, zero, fx_low)


def residuals(lo, hi, field, coefs, use):
    faces, over = coefs[:2]
    group = min(hi - lo, 8 if field.shape[1] <= 16 else 4)

    def body(turn, carry):
        start = lo + turn * group
        xs = list(carry) + [field[start + j + 1] for j in range(group)]
        results = []
        for j in range(group):
            i, x = start + j, xs[j + 1]
            along_x = faces[0, i] * xs[j + 2] + faces[1, i] * xs[j]
            along_y = faces[2, i] * up(x, 0) + faces[3, i] * down(x, 0)
            along_z = faces[4, i] * up(x, 1) + faces[5, i] * down(x, 1)
            results.append(((over[i] - x) + along_x) + (along_y + along_z))
        use(start, xs[1:-1], results)
        return xs[-2], xs[-1]

    low = field[lo - 1] if lo > 0 else jnp.zeros(field.shape[1:], F32)
    lax.fori_loop(0, (hi - lo) // group, body, (low, field[lo]))


def sweep(lo, hi, field, step, coefs, keep, gain):
    def use(start, xs, results):
        moves = [gain * z for z in results]
        if keep is not None:
            moves = [keep * step[start + j] + move for j, move in enumerate(moves)]
        for j, (x, move) in enumerate(zip(xs, moves)):
            step[start + j] = move
            field[start + j] = x + move

    residuals(lo, hi, field, coefs, use)


def pairs_rows(out_rows, in_rows):
    r = lax.broadcasted_iota(jnp.int32, (out_rows, in_rows), 0)
    c = lax.broadcasted_iota(jnp.int32, (out_rows, in_rows), 1)
    return jnp.where((c == 2 * r) | (c == 2 * r + 1), 1.0, 0.0).astype(F32)


def pairs_lanes(in_lanes, out_lanes, shift=0):
    r = lax.broadcasted_iota(jnp.int32, (in_lanes, out_lanes), 0)
    c = lax.broadcasted_iota(jnp.int32, (in_lanes, out_lanes), 1) - shift
    return jnp.where((r == 2 * c) | (r == 2 * c + 1), 1.0, 0.0).astype(F32)


def dot(a, b):
    return jnp.dot(a, b, precision=lax.Precision.HIGHEST, preferred_element_type=F32)


def full_smooth(n, field, step, coefs, zero_start):
    if not zero_start:
        sweep(0, n, field, step, coefs, None, 1.0 / THETA)
    for keep, gain in chebyshev():
        sweep(0, n, field, step, coefs, keep, gain)


def coarse_cycle(levels, level):
    n, cond, right, field, step, coefs, temp, scale = levels[level]
    build(cond, n, right, coefs, field, step, scale)
    field[n] = jnp.zeros(field.shape[1:], F32)
    full_smooth(n, field, step, coefs, True)
    if level == len(levels) - 1:
        full_smooth(n, field, step, coefs, False)
        return
    half, below, below_right, below_field = n // 2, *levels[level + 1][1:4]
    rows, lanes = field.shape[1:]
    out_rows, out_lanes = below_field.shape[1:]

    def keep_resid(start, xs, results):
        for j, z in enumerate(results):
            temp[start + j] = z * coefs[2][start + j]

    residuals(0, n, field, coefs, keep_resid)
    merge = pairs_rows(half * out_rows, half * rows)
    squeeze = pairs_lanes(lanes, out_lanes)
    for source, target in ((temp, below_right), (cond, below)):
        both = source[...].reshape(half, 2, rows, lanes)
        both = (both[:, 0] + both[:, 1]).reshape(half * rows, lanes)
        target[...] = (dot(dot(merge, both), squeeze) * 0.125).reshape(half, out_rows, out_lanes)
    coarse_cycle(levels, level + 1)
    error = below_field[pl.ds(0, half)].reshape(half * out_rows, out_lanes)
    split = lax.broadcasted_iota(jnp.int32, (half * rows, half * out_rows), 0) // 2
    split = jnp.where(
        split == lax.broadcasted_iota(jnp.int32, (half * rows, half * out_rows), 1), 1.0, 0.0
    )
    spread = lax.broadcasted_iota(jnp.int32, (out_lanes, lanes), 1) // 2
    spread = jnp.where(
        spread == lax.broadcasted_iota(jnp.int32, (out_lanes, lanes), 0), 1.0, 0.0
    )
    error = dot(dot(split, error), spread).reshape(half, rows, lanes)
    for i in range(half):
        field[2 * i] = field[2 * i] + error[i]
        field[2 * i + 1] = field[2 * i + 1] + error[i]
    full_smooth(n, field, step, coefs, False)


def pack_block(values):
    bx, by, bz = values.shape
    rows = bx // 2 * by // 2
    both = values.reshape(bx // 2, 2, by, bz)
    both = (both[:, 0] + both[:, 1]).reshape(bx // 2 * by, bz)
    both = dot(pairs_rows(rows, 2 * rows), both)
    low = dot(both[:rows // 2], pairs_lanes(bz, bz))
    high = dot(both[rows // 2:], pairs_lanes(bz, bz, bz // 2))
    return ((low + high) * 0.125).reshape(bx // 4, by // 2, bz)


def partner_groups(sizes, places):
    groups = []
    for which in (1, 2, 0):
        axis, at, count = ("gx", "gy", "gz")[which], places[which], sizes[which]
        groups.append([(axis, lax.rem(at + off, count)) for off in range(1, count)])
    return groups


def greet(groups):
    barrier = pltpu.get_barrier_semaphore()
    for group in groups:
        for axis, other in group:
            pl.semaphore_signal(barrier, inc=1, device_id={axis: other}, device_id_type=MESH)


def await_greetings(groups):
    pl.semaphore_wait(pltpu.get_barrier_semaphore(), sum(len(group) for group in groups))


def gather_stages(places, groups, full, sems_out, sems_in):
    ix, iy, iz = places
    slots = iter(range(sems_out.shape[0]))

    def copies(group, source):
        made = []
        for axis, other in group:
            slot = next(slots)
            made.append(
                pltpu.make_async_remote_copy(
                    src_ref=source,
                    dst_ref=source,
                    send_sem=sems_out.at[slot],
                    recv_sem=sems_in.at[slot],
                    device_id={axis: other},
                    device_id_type=MESH,
                )
            )
        return made

    along_y = copies(groups[0], full.at[ix, iz, iy])
    along_z = copies(groups[1], full.at[ix, iz])
    count = full.shape[1]
    columns = [
        copies(groups[2], full.at[ix, lax.rem(iz + count - off, count)]) for off in range(count)
    ]
    return along_y, along_z, columns


def middle_stage(stages):
    end_stage(stages[0])
    start_stage(stages[1])
    start_stage(stages[2][0])


def last_stage(stages):
    for copy, column in zip(stages[1], stages[2][1:]):
        copy.wait_recv()
        start_stage(column)


def end_gather(stages):
    for column in stages[2]:
        end_stage(column)
    for copy in sum(stages[2], stages[0] + stages[1]):
        copy.wait_send()


def start_stage(stage):
    for copy in stage:
        copy.start()


def end_stage(stage):
    for copy in stage:
        copy.wait_recv()


def halo_kernel(
    sizes, heat, material, table, ext, full,
    pack, got, sems_out, sems_in, gather_out, gather_in,
):
    nx, ny, nz = sizes
    places = ix, iy, iz = tuple(lax.axis_index(axis) for axis in ("gx", "gy", "gz"))
    bx, by, bz = heat.shape
    ext[...] = jnp.zeros(ext.shape, F32)
    got[...] = jnp.zeros(got.shape, F32)
    groups = partner_groups(sizes, places)
    greet(groups)
    own = (pl.ds(HX, bx), pl.ds(HY, by), pl.ds(0, bz))
    ext[(0, *own)] = heat[...]
    cond = jnp.zeros((bx, by, bz), F32)
    for which in range(MATERIALS):
        cond = cond + jnp.where(material[...] == which, table[which], 0.0)
    ext[(1, *own)] = cond
    lane = lax.broadcasted_iota(jnp.int32, (by, bz), 1)
    for part in range(2):
        low = jnp.zeros((by, bz), F32)
        high = low
        for x in range(bx):
            v = ext[part, HX + x, pl.ds(HY, by), pl.ds(0, bz)]
            mine = (lane >= HZ * x) & (lane < HZ * (x + 1))
            low = jnp.where(mine, pltpu.roll(v, (HZ * x) % bz, 1), low)
            high = jnp.where(mine, pltpu.roll(v, HZ * (x + 1) % bz, 1), high)
        pack[0, part] = low
        pack[1, part] = high

    sides = []
    for axis, at, count in (("gx", ix, nx), ("gy", iy, ny), ("gz", iz, nz)):
        sides.append((axis, at > 0, at - 1))
        sides.append((axis, at < count - 1, at + 1))

    def send(which, slot, low_source, low_target, high_source, high_target):
        copies = []
        for turn, (source, target) in enumerate(
            ((low_source, low_target), (high_source, high_target))
        ):
            axis, there, other = sides[which + turn]
            copy = pltpu.make_async_remote_copy(
                src_ref=source,
                dst_ref=target,
                send_sem=sems_out.at[slot + turn],
                recv_sem=sems_in.at[slot + turn],
                device_id={axis: other},
                device_id_type=MESH,
            )
            copies.append((there, copy))
            pl.when(there)(copy.start)
        return copies

    def receive(copies):
        pl.when(copies[0][0])(copies[1][1].wait_recv)
        pl.when(copies[1][0])(copies[0][1].wait_recv)

    def rows(start):
        return ext.at[:, pl.ds(HX, bx), pl.ds(start, HY), pl.ds(0, bz)]

    def planes(start):
        return ext.at[:, pl.ds(start, HX)]

    middle = pl.ds(HY, by)
    full[ix, iz, iy] = pack_block(cond)
    stages = gather_stages(places, groups, full, gather_out, gather_in)
    await_greetings(groups)
    start_stage(stages[0])
    sent = [
        send(4, 4, pack.at[0], got.at[1, :, middle], pack.at[1], got.at[0, :, middle]),
        send(2, 2, rows(HY), rows(HY + by), rows(by), rows(0)),
    ]
    receive(sent[0])

    def edges(start):
        return got.at[:, :, pl.ds(start, HY)]

    sent.append(send(2, 6, edges(HY), edges(HY + by), edges(by), edges(0)))
    middle_stage(stages)
    receive(sent[2])
    lane = lax.broadcasted_iota(jnp.int32, (ext.shape[2], bz), 1)
    for part in range(2):
        left, right = got[0, part], got[1, part]
        for x in range(bx):
            v = jnp.where(lane < HZ, pltpu.roll(right, (bz - HZ * x) % bz, 1), 0.0)
            v = jnp.where(lane >= bz - HZ, pltpu.roll(left, (2 * bz - HZ * (x + 1)) % bz, 1), v)
            ext[part, HX + x, :, pl.ds(bz, bz)] = v
    receive(sent[1])
    sent.append(send(0, 0, planes(HX), planes(HX + bx), planes(bx), planes(0)))
    last_stage(stages)
    receive(sent[3])
    for copies in sent:
        for there, copy in copies:
            pl.when(there)(copy.wait_send)
    end_gather(stages)


def pre_kernel(ext, faces, over, field, packed, diagonal, step, temp):
    n = ext.shape[1]
    bx, by, bz = n - 2 * HX, ext.shape[2] - 2 * HY, ext.shape[3] // 2
    right, cond = ext.at[0], ext.at[1]
    coefs = (faces, over, diagonal)
    build(cond, n, right, coefs, field, step, 1.0, True)
    for keep, gain in chebyshev():
        sweep(2, n - 2, field, step, coefs, keep, gain)

    def keep_resid(start, xs, results):
        for j, z in enumerate(results):
            i = start + j
            temp[i - HX] = (z * diagonal[i])[HY:HY + by, :bz]

    residuals(HX, HX + bx, field, coefs, keep_resid)
    packed[...] = pack_block(temp[...])


def gather_kernel(sizes, block, full, sems_out, sems_in):
    places = ix, iy, iz = tuple(lax.axis_index(axis) for axis in ("gx", "gy", "gz"))
    groups = partner_groups(sizes, places)
    greet(groups)
    full[ix, iz, iy] = block[...]
    await_greetings(groups)
    stages = gather_stages(places, groups, full, sems_out, sems_in)
    start_stage(stages[0])
    middle_stage(stages)
    last_stage(stages)
    end_gather(stages)


def post_kernel(sizes, faces, over, start, full_right, full_cond, out, *scratch):
    nx, ny, nz = sizes
    ix, iy, iz = lax.axis_index("gx"), lax.axis_index("gy"), lax.axis_index("gz")
    n = start.shape[0]
    bx, by, bz = out.shape
    field, step = scratch[:2]
    levels, place, scale = [], 2, 0.25
    pad = HX // 2
    for level in range(1, LEVELS + 1):
        cond, right, whole, moves, temp, *coefs = scratch[place:place + 8]
        place += 8
        planes = cond.shape[0]
        values = whole.at[pl.ds(pad, planes + 1)] if level == 1 else whole
        if level == 1:
            coarse = whole
        levels.append((planes, cond, right, values, moves, tuple(coefs), temp, scale))
        scale *= 0.25
    _, cond, right = levels[0][:3]

    cx, cy = bx // 2, by // 2
    lane = lax.broadcasted_iota(jnp.int32, (cy, bz), 1)

    for full, target in ((full_right, right), (full_cond, cond)):
        for px in range(nx):
            for q in range(nz // 2):
                for py in range(ny):
                    for i in range(cx // 2):
                        one, two = full[px, 2 * q, py, i], full[px, 2 * q + 1, py, i]
                        place = (pl.ds(py * cy, cy), pl.ds(q * bz, bz))
                        low = jnp.where(lane < bz // 2, one, pltpu.roll(two, bz // 2, 1))
                        high = jnp.where(lane < bz // 2, pltpu.roll(one, bz // 2, 1), two)
                        target[(px * cx + i, *place)] = low
                        target[(px * cx + cx // 2 + i, *place)] = high
    zero = jnp.zeros((pad, *coarse.shape[1:]), F32)
    coarse[pl.ds(0, pad)] = zero
    coarse[pl.ds(coarse.shape[0] - pad, pad)] = zero
    coarse_cycle(levels, 0)

    rows, lanes = start.shape[1:]
    crows, clanes = coarse.shape[1:]
    r = lax.broadcasted_iota(jnp.int32, (rows, crows), 0)
    c = lax.broadcasted_iota(jnp.int32, (rows, crows), 1)
    fine = 2 * (c - cy * iy) + HY
    split = jnp.where((r == fine) | (r == fine + 1), 1.0, 0.0).astype(F32)
    r = lax.broadcasted_iota(jnp.int32, (clanes, lanes), 0)
    c = lax.broadcasted_iota(jnp.int32, (clanes, lanes), 1)
    c = jnp.where(c >= lanes - HZ, c - lanes, c)
    fine = 2 * (r - bz // 2 * iz)
    spread = jnp.where((c == fine) | (c == fine + 1), 1.0, 0.0).astype(F32)

    window = coarse[pl.ds(cx * ix, n // 2)].reshape(n // 2 * crows, clanes)
    window = dot(window, spread).reshape(n // 2, crows, lanes)
    for i in range(n // 2):
        error = dot(split, window[i])
        field[2 * i] = start[2 * i] + error
        field[2 * i + 1] = start[2 * i + 1] + error
    coefs = (faces, over)
    low = HX - 2
    sweep(low, n - low, field, step, coefs, None, 1.0 / THETA)
    for turn, (keep, gain) in enumerate(chebyshev()):
        low = HX - 2 if turn == 0 else HX
        sweep(low, n - low, field, step, coefs, keep, gain)
    for i in range(bx):
        out[i] = field[HX + i, HY:HY + by, :bz]


def local(sizes, heat, material, table):
    nx, ny, nz = sizes
    bx, by, bz = heat.shape
    n, rows, lanes = bx + 2 * HX, by + 2 * HY, 2 * bz
    vmem = pl.BlockSpec(memory_space=pltpu.VMEM)
    smem = pl.BlockSpec(memory_space=pltpu.SMEM)
    limit = 30 * 1024 * 1024
    array = jax.ShapeDtypeStruct
    count = ny - 1 + nz - 1 + (nx - 1) * nz
    coarse = array((nx, nz, ny, bx // 4, by // 2, bz), F32)
    dma = pltpu.SemaphoreType.DMA
    ext, full_cond = pl.pallas_call(
        functools.partial(halo_kernel, sizes),
        out_shape=[array((2, n, rows, lanes), F32), coarse],
        in_specs=[vmem, vmem, smem],
        out_specs=[vmem, vmem],
        scratch_shapes=[
            pltpu.VMEM((2, 2, by, bz), F32),
            pltpu.VMEM((2, 2, rows, bz), F32),
            dma((8,)),
            dma((8,)),
            dma((count,)),
            dma((count,)),
        ],
        compiler_params=pltpu.CompilerParams(
            collective_id=0, has_side_effects=True, vmem_limit_bytes=limit
        ),
    )(heat, material, table)
    fine = pltpu.VMEM((n, rows, lanes), F32)
    faces, over, start, packed = pl.pallas_call(
        pre_kernel,
        out_shape=[
            array((6, n, rows, lanes), F32),
            array((n, rows, lanes), F32),
            array((n, rows, lanes), F32),
            array((bx // 4, by // 2, bz), F32),
        ],
        in_specs=[vmem],
        out_specs=[vmem] * 4,
        scratch_shapes=[fine] * 2 + [pltpu.VMEM((bx, by, bz), F32)],
        compiler_params=pltpu.CompilerParams(vmem_limit_bytes=limit),
    )(ext)
    full_right = pl.pallas_call(
        functools.partial(gather_kernel, sizes),
        out_shape=coarse,
        in_specs=[vmem],
        out_specs=vmem,
        scratch_shapes=[pltpu.SemaphoreType.DMA((count,)), pltpu.SemaphoreType.DMA((count,))],
        compiler_params=pltpu.CompilerParams(
            collective_id=1, has_side_effects=True, vmem_limit_bytes=limit
        ),
    )(packed)
    scratch = [fine] * 2
    for level in range(1, LEVELS + 1):
        shape = (bx * nx >> level, by * ny >> level, max(bz * nz >> level, 128))
        extra = HX if level == 1 else 1
        scratch += [pltpu.VMEM(shape, F32)] * 2
        scratch += [pltpu.VMEM((shape[0] + extra, *shape[1:]), F32)]
        scratch += [pltpu.VMEM(shape, F32)] * 2
        scratch += [pltpu.VMEM((6, *shape), F32)]
        scratch += [pltpu.VMEM(shape, F32)] * 2
    return pl.pallas_call(
        functools.partial(post_kernel, sizes),
        out_shape=array(heat.shape, F32),
        in_specs=[vmem] * 5,
        out_specs=vmem,
        scratch_shapes=scratch,
        compiler_params=pltpu.CompilerParams(vmem_limit_bytes=limit),
    )(faces, over, start, full_right, full_cond)


def with_halo(block, sides):
    for axis, dim in sides:
        count = lax.axis_size(axis)
        forward = [(i, i + 1) for i in range(count - 1)]
        backward = [(target, source) for source, target in forward]
        low = lax.ppermute(
            lax.slice_in_dim(block, block.shape[dim] - 1, None, axis=dim), axis, forward
        )
        high = lax.ppermute(lax.slice_in_dim(block, 0, 1, axis=dim), axis, backward)
        block = jnp.concatenate([low, block, high], axis=dim)
    return block


def neighbours(block):
    padded = with_halo(block, (("gx", 0), ("gy", 1), ("gz", 2)))
    return (
        padded[2:, 1:-1, 1:-1],
        padded[:-2, 1:-1, 1:-1],
        padded[1:-1, 2:, 1:-1],
        padded[1:-1, :-2, 1:-1],
        padded[1:-1, 1:-1, 2:],
        padded[1:-1, 1:-1, :-2],
    )


def large_smooth(right, start, faces, diag, scale):
    inverse = 1.0 / (scale * diag)
    if start is None:
        step = inverse * right / THETA
        field = step
    else:
        step = inverse * large_resid(right, start, faces, diag, scale) / THETA
        field = start + step
    for keep, gain in chebyshev():
        step = keep * step + gain * inverse * large_resid(right, field, faces, diag, scale)
        field = field + step
    return field


def large_resid(right, field, faces, diag, scale):
    total = sum(face * near for face, near in zip(faces, neighbours(field)))
    return right - scale * (diag * field - total)


def restrict(field):
    sx, sy, sz = field.shape
    return field.reshape(sx // 2, 2, sy // 2, 2, sz // 2, 2).mean(axis=(1, 3, 5))


def large_cycle(right, cond, level, scale):
    faces = []
    for other in neighbours(cond):
        other = jnp.where(other > 0.0, other, cond)
        faces.append(2.0 * cond * other / (cond + other))
    diag = sum(faces)
    field = large_smooth(right, None, faces, diag, scale)
    if level < LEVELS:
        resid = large_resid(right, field, faces, diag, scale)
        error = large_cycle(restrict(resid), restrict(cond), level + 1, scale * 0.25)
        for dim in range(3):
            error = jnp.repeat(error, 2, dim)
        field = field + error
    return large_smooth(right, field, faces, diag, scale)


def large(heat, material, table):
    cond = jnp.zeros(heat.shape, F32)
    for which in range(MATERIALS):
        cond = cond + jnp.where(material == which, table[which], 0.0)
    return large_cycle(heat, cond, 0, 1.0)


def solution(mesh):
    sizes = tuple(mesh.shape[axis] for axis in ("gx", "gy", "gz"))

    def run(heat, material, table):
        small = heat.size // 8 <= 1 << 18
        body = functools.partial(local, sizes) if small else large
        spec = P("gx", "gy", "gz")
        return jax.shard_map(
            body, mesh=mesh, in_specs=(spec, spec, P()), out_specs=spec, check_vma=False
        )(heat, material, table)

    return run
```

```python
import functools

import jax
import jax.numpy as jnp
from jax import lax
from jax.experimental import pallas as pl
from jax.experimental.pallas import tpu as pltpu
from jax.sharding import PartitionSpec as P

DEGREE = 3
LEVELS = 3
MATERIALS = 3

LOW = 0.3
HIGH = 2.0
THETA = 0.5 * (HIGH + LOW)
DELTA = 0.5 * (HIGH - LOW)
SIGMA = THETA / DELTA

HX = 6
HY = 8
HZ = 8
MESH = pl.DeviceIdType.MESH
F32 = jnp.float32


def chebyshev():
    rho = 1.0 / SIGMA
    pairs = []
    for _ in range(DEGREE - 1):
        new = 1.0 / (2.0 * SIGMA - rho)
        pairs.append((new * rho, 2.0 * new / DELTA))
        rho = new
    return pairs


def up(v, axis):
    return pltpu.roll(v, v.shape[axis] - 1, axis)


def down(v, axis):
    return pltpu.roll(v, 1, axis)


def harmonic(a, b):
    return 2.0 * a * b / jnp.maximum(a + b, 1e-30)


def build(cond, n, right, coefs, field, step, scale, ring=False):
    faces, over, diagonal = coefs
    shape = cond.shape[1:]
    row = lax.broadcasted_iota(jnp.int32, shape, 0)
    lane = lax.broadcasted_iota(jnp.int32, shape, 1)

    def plane(i, k, k_low, k_high, fx_low):
        ky_high = jnp.where(row == shape[0] - 1, 0.0, up(k, 0))
        ky_low = jnp.where(row == 0, 0.0, down(k, 0))
        kz_high, kz_low = up(k, 1), down(k, 1)
        if not ring:
            kz_high = jnp.where(lane == shape[1] - 1, 0.0, kz_high)
            kz_low = jnp.where(lane == 0, 0.0, kz_low)
        fx, fy, fz = harmonic(k, k_high), harmonic(k, ky_high), harmonic(k, kz_high)
        missing = jnp.zeros(shape, F32)
        for other in (k_low, k_high, ky_low, ky_high, kz_low, kz_high):
            missing = missing + jnp.where(other > 0.0, 0.0, k)
        fy_low, fz_low = down(fy, 0), down(fz, 1)
        diag = fx + fx_low + fy + fy_low + fz + fz_low + missing
        inverse = jnp.where(k > 0.0, 1.0 / jnp.maximum(diag, 1e-30), 0.0)
        for side, face in enumerate((fx, fx_low, fy, fy_low, fz, fz_low)):
            faces[side, i] = face * inverse
        value = inverse * (1.0 / scale) * right[i]
        over[i] = value
        diagonal[i] = diag * scale
        field[i] = value * (1.0 / THETA)
        step[i] = value * (1.0 / THETA)
        return fx

    def body(i, carry):
        k, k_low, fx_low = carry
        k_high = cond[i + 1]
        fx = plane(i, k, k_low, k_high, fx_low)
        return k_high, k, fx

    zero = jnp.zeros(shape, F32)
    unroll = True if n <= 8 else 3
    k, k_low, fx_low = lax.fori_loop(0, n - 1, body, (cond[0], zero, zero), unroll=unroll)
    plane(n - 1, k, k_low, zero, fx_low)


def residuals(lo, hi, field, coefs, use):
    faces, over = coefs[:2]
    group = min(hi - lo, 4 if (hi - lo) % 8 else 8)

    def body(turn, carry):
        start = lo + turn * group
        xs = list(carry) + [field[start + j + 1] for j in range(group)]
        results = []
        for j in range(group):
            i, x = start + j, xs[j + 1]
            along_x = faces[0, i] * xs[j + 2] + faces[1, i] * xs[j]
            along_y = faces[2, i] * up(x, 0) + faces[3, i] * down(x, 0)
            along_z = faces[4, i] * up(x, 1) + faces[5, i] * down(x, 1)
            results.append(((over[i] - x) + along_x) + (along_y + along_z))
        use(start, xs[1:-1], results)
        return xs[-2], xs[-1]

    low = field[lo - 1] if lo > 0 else jnp.zeros(field.shape[1:], F32)
    lax.fori_loop(0, (hi - lo) // group, body, (low, field[lo]))


def sweep(lo, hi, field, step, coefs, keep, gain):
    def use(start, xs, results):
        moves = [gain * z for z in results]
        if keep is not None:
            moves = [keep * step[start + j] + move for j, move in enumerate(moves)]
        for j, (x, move) in enumerate(zip(xs, moves)):
            step[start + j] = move
            field[start + j] = x + move

    residuals(lo, hi, field, coefs, use)


def pairs_rows(out_rows, in_rows):
    r = lax.broadcasted_iota(jnp.int32, (out_rows, in_rows), 0)
    c = lax.broadcasted_iota(jnp.int32, (out_rows, in_rows), 1)
    return jnp.where((c == 2 * r) | (c == 2 * r + 1), 1.0, 0.0).astype(F32)


def pairs_lanes(in_lanes, out_lanes, shift=0):
    r = lax.broadcasted_iota(jnp.int32, (in_lanes, out_lanes), 0)
    c = lax.broadcasted_iota(jnp.int32, (in_lanes, out_lanes), 1) - shift
    return jnp.where((r == 2 * c) | (r == 2 * c + 1), 1.0, 0.0).astype(F32)


def dot(a, b):
    return jnp.dot(a, b, precision=lax.Precision.HIGHEST, preferred_element_type=F32)


def full_smooth(n, field, step, coefs, zero_start):
    if not zero_start:
        sweep(0, n, field, step, coefs, None, 1.0 / THETA)
    for keep, gain in chebyshev():
        sweep(0, n, field, step, coefs, keep, gain)


def coarse_cycle(levels, level):
    n, cond, right, field, step, coefs, temp, scale = levels[level]
    build(cond, n, right, coefs, field, step, scale)
    field[n] = jnp.zeros(field.shape[1:], F32)
    full_smooth(n, field, step, coefs, True)
    if level == len(levels) - 1:
        full_smooth(n, field, step, coefs, False)
        return
    half, below, below_right, below_field = n // 2, *levels[level + 1][1:4]
    rows, lanes = field.shape[1:]
    out_rows, out_lanes = below_field.shape[1:]

    def keep_resid(start, xs, results):
        for j, z in enumerate(results):
            temp[start + j] = z * coefs[2][start + j]

    residuals(0, n, field, coefs, keep_resid)
    merge = pairs_rows(half * out_rows, half * rows)
    squeeze = pairs_lanes(lanes, out_lanes)
    for source, target in ((temp, below_right), (cond, below)):
        both = source[...].reshape(half, 2, rows, lanes)
        both = (both[:, 0] + both[:, 1]).reshape(half * rows, lanes)
        target[...] = (dot(dot(merge, both), squeeze) * 0.125).reshape(half, out_rows, out_lanes)
    coarse_cycle(levels, level + 1)
    error = below_field[pl.ds(0, half)].reshape(half * out_rows, out_lanes)
    split = lax.broadcasted_iota(jnp.int32, (half * rows, half * out_rows), 0) // 2
    split = jnp.where(
        split == lax.broadcasted_iota(jnp.int32, (half * rows, half * out_rows), 1), 1.0, 0.0
    )
    spread = lax.broadcasted_iota(jnp.int32, (out_lanes, lanes), 1) // 2
    spread = jnp.where(
        spread == lax.broadcasted_iota(jnp.int32, (out_lanes, lanes), 0), 1.0, 0.0
    )
    error = dot(dot(split, error), spread).reshape(half, rows, lanes)
    for i in range(half):
        field[2 * i] = field[2 * i] + error[i]
        field[2 * i + 1] = field[2 * i + 1] + error[i]
    full_smooth(n, field, step, coefs, False)


def pack_block(values):
    bx, by, bz = values.shape
    rows = bx // 2 * by // 2
    both = values.reshape(bx // 2, 2, by, bz)
    both = (both[:, 0] + both[:, 1]).reshape(bx // 2 * by, bz)
    both = dot(pairs_rows(rows, 2 * rows), both)
    low = dot(both[:rows // 2], pairs_lanes(bz, bz))
    high = dot(both[rows // 2:], pairs_lanes(bz, bz, bz // 2))
    return ((low + high) * 0.125).reshape(bx // 4, by // 2, bz)


def partner_groups(sizes, places):
    groups = []
    for which in (1, 2, 0):
        axis, at, count = ("gx", "gy", "gz")[which], places[which], sizes[which]
        groups.append([(axis, lax.rem(at + off, count)) for off in range(1, count)])
    return groups


def greet(groups):
    barrier = pltpu.get_barrier_semaphore()
    for group in groups:
        for axis, other in group:
            pl.semaphore_signal(barrier, inc=1, device_id={axis: other}, device_id_type=MESH)


def await_greetings(groups):
    pl.semaphore_wait(pltpu.get_barrier_semaphore(), sum(len(group) for group in groups))


def gather_stages(places, groups, full, sems_out, sems_in):
    ix, iy, iz = places
    slots = iter(range(sems_out.shape[0]))

    def copies(group, source):
        made = []
        for axis, other in group:
            slot = next(slots)
            made.append(
                pltpu.make_async_remote_copy(
                    src_ref=source,
                    dst_ref=source,
                    send_sem=sems_out.at[slot],
                    recv_sem=sems_in.at[slot],
                    device_id={axis: other},
                    device_id_type=MESH,
                )
            )
        return made

    along_y = copies(groups[0], full.at[ix, iz, iy])
    along_z = copies(groups[1], full.at[ix, iz])
    count = full.shape[1]
    columns = [
        copies(groups[2], full.at[ix, lax.rem(iz + count - off, count)]) for off in range(count)
    ]
    return along_y, along_z, columns


def middle_stage(stages):
    end_stage(stages[0])
    start_stage(stages[1])
    start_stage(stages[2][0])


def last_stage(stages):
    for copy, column in zip(stages[1], stages[2][1:]):
        copy.wait_recv()
        start_stage(column)


def end_gather(stages):
    for column in stages[2]:
        end_stage(column)
    for copy in sum(stages[2], stages[0] + stages[1]):
        copy.wait_send()


def start_stage(stage):
    for copy in stage:
        copy.start()


def end_stage(stage):
    for copy in stage:
        copy.wait_recv()


def halo_kernel(
    sizes, heat, material, table, ext, full,
    pack, got, sems_out, sems_in, gather_out, gather_in,
):
    nx, ny, nz = sizes
    places = ix, iy, iz = tuple(lax.axis_index(axis) for axis in ("gx", "gy", "gz"))
    bx, by, bz = heat.shape
    ext[...] = jnp.zeros(ext.shape, F32)
    got[...] = jnp.zeros(got.shape, F32)
    groups = partner_groups(sizes, places)
    greet(groups)
    own = (pl.ds(HX, bx), pl.ds(HY, by), pl.ds(0, bz))
    ext[(0, *own)] = heat[...]
    cond = jnp.zeros((bx, by, bz), F32)
    for which in range(MATERIALS):
        cond = cond + jnp.where(material[...] == which, table[which], 0.0)
    ext[(1, *own)] = cond
    lane = lax.broadcasted_iota(jnp.int32, (by, bz), 1)
    for part in range(2):
        low = jnp.zeros((by, bz), F32)
        high = low
        for x in range(bx):
            v = ext[part, HX + x, pl.ds(HY, by), pl.ds(0, bz)]
            mine = (lane >= HZ * x) & (lane < HZ * (x + 1))
            low = jnp.where(mine, pltpu.roll(v, (HZ * x) % bz, 1), low)
            high = jnp.where(mine, pltpu.roll(v, HZ * (x + 1) % bz, 1), high)
        pack[0, part] = low
        pack[1, part] = high

    sides = []
    for axis, at, count in (("gx", ix, nx), ("gy", iy, ny), ("gz", iz, nz)):
        sides.append((axis, at > 0, at - 1))
        sides.append((axis, at < count - 1, at + 1))

    def send(which, slot, low_source, low_target, high_source, high_target):
        copies = []
        for turn, (source, target) in enumerate(
            ((low_source, low_target), (high_source, high_target))
        ):
            axis, there, other = sides[which + turn]
            copy = pltpu.make_async_remote_copy(
                src_ref=source,
                dst_ref=target,
                send_sem=sems_out.at[slot + turn],
                recv_sem=sems_in.at[slot + turn],
                device_id={axis: other},
                device_id_type=MESH,
            )
            copies.append((there, copy))
            pl.when(there)(copy.start)
        return copies

    def receive(copies):
        pl.when(copies[0][0])(copies[1][1].wait_recv)
        pl.when(copies[1][0])(copies[0][1].wait_recv)

    def rows(start):
        return ext.at[:, pl.ds(HX, bx), pl.ds(start, HY), pl.ds(0, bz)]

    def planes(start):
        return ext.at[:, pl.ds(start, HX)]

    middle = pl.ds(HY, by)
    full[ix, iz, iy] = pack_block(cond)
    stages = gather_stages(places, groups, full, gather_out, gather_in)
    await_greetings(groups)
    start_stage(stages[0])
    sent = [
        send(4, 4, pack.at[0], got.at[1, :, middle], pack.at[1], got.at[0, :, middle]),
        send(2, 2, rows(HY), rows(HY + by), rows(by), rows(0)),
    ]
    receive(sent[0])

    def edges(start):
        return got.at[:, :, pl.ds(start, HY)]

    sent.append(send(2, 6, edges(HY), edges(HY + by), edges(by), edges(0)))
    middle_stage(stages)
    receive(sent[2])
    lane = lax.broadcasted_iota(jnp.int32, (ext.shape[2], bz), 1)
    for part in range(2):
        left, right = got[0, part], got[1, part]
        for x in range(bx):
            v = jnp.where(lane < HZ, pltpu.roll(right, (bz - HZ * x) % bz, 1), 0.0)
            v = jnp.where(lane >= bz - HZ, pltpu.roll(left, (2 * bz - HZ * (x + 1)) % bz, 1), v)
            ext[part, HX + x, :, pl.ds(bz, bz)] = v
    receive(sent[1])
    sent.append(send(0, 0, planes(HX), planes(HX + bx), planes(bx), planes(0)))
    last_stage(stages)
    receive(sent[3])
    for copies in sent:
        for there, copy in copies:
            pl.when(there)(copy.wait_send)
    end_gather(stages)


def pre_kernel(ext, faces, over, field, packed, diagonal, step, temp):
    n = ext.shape[1]
    bx, by, bz = n - 2 * HX, ext.shape[2] - 2 * HY, ext.shape[3] // 2
    right, cond = ext.at[0], ext.at[1]
    coefs = (faces, over, diagonal)
    build(cond, n, right, coefs, field, step, 1.0, True)
    for keep, gain in chebyshev():
        sweep(2, n - 2, field, step, coefs, keep, gain)

    def keep_resid(start, xs, results):
        for j, z in enumerate(results):
            i = start + j
            temp[i - HX] = (z * diagonal[i])[HY:HY + by, :bz]

    residuals(HX, HX + bx, field, coefs, keep_resid)
    packed[...] = pack_block(temp[...])


def gather_kernel(sizes, block, full, sems_out, sems_in):
    places = ix, iy, iz = tuple(lax.axis_index(axis) for axis in ("gx", "gy", "gz"))
    groups = partner_groups(sizes, places)
    greet(groups)
    full[ix, iz, iy] = block[...]
    await_greetings(groups)
    stages = gather_stages(places, groups, full, sems_out, sems_in)
    start_stage(stages[0])
    middle_stage(stages)
    last_stage(stages)
    end_gather(stages)


def post_kernel(sizes, faces, over, start, full_right, full_cond, out, *scratch):
    nx, ny, nz = sizes
    ix, iy, iz = lax.axis_index("gx"), lax.axis_index("gy"), lax.axis_index("gz")
    n = start.shape[0]
    bx, by, bz = out.shape
    field, step = scratch[:2]
    levels, place, scale = [], 2, 0.25
    pad = HX // 2
    for level in range(1, LEVELS + 1):
        cond, right, whole, moves, temp, *coefs = scratch[place:place + 8]
        place += 8
        planes = cond.shape[0]
        values = whole.at[pl.ds(pad, planes + 1)] if level == 1 else whole
        if level == 1:
            coarse = whole
        levels.append((planes, cond, right, values, moves, tuple(coefs), temp, scale))
        scale *= 0.25
    _, cond, right = levels[0][:3]

    cx, cy = bx // 2, by // 2
    lane = lax.broadcasted_iota(jnp.int32, (cy, bz), 1)

    for full, target in ((full_right, right), (full_cond, cond)):
        for px in range(nx):
            for q in range(nz // 2):
                for py in range(ny):
                    for i in range(cx // 2):
                        one, two = full[px, 2 * q, py, i], full[px, 2 * q + 1, py, i]
                        place = (pl.ds(py * cy, cy), pl.ds(q * bz, bz))
                        low = jnp.where(lane < bz // 2, one, pltpu.roll(two, bz // 2, 1))
                        high = jnp.where(lane < bz // 2, pltpu.roll(one, bz // 2, 1), two)
                        target[(px * cx + i, *place)] = low
                        target[(px * cx + cx // 2 + i, *place)] = high
    zero = jnp.zeros((pad, *coarse.shape[1:]), F32)
    coarse[pl.ds(0, pad)] = zero
    coarse[pl.ds(coarse.shape[0] - pad, pad)] = zero
    coarse_cycle(levels, 0)

    rows, lanes = start.shape[1:]
    crows, clanes = coarse.shape[1:]
    r = lax.broadcasted_iota(jnp.int32, (rows, crows), 0)
    c = lax.broadcasted_iota(jnp.int32, (rows, crows), 1)
    fine = 2 * (c - cy * iy) + HY
    split = jnp.where((r == fine) | (r == fine + 1), 1.0, 0.0).astype(F32)
    r = lax.broadcasted_iota(jnp.int32, (clanes, lanes), 0)
    c = lax.broadcasted_iota(jnp.int32, (clanes, lanes), 1)
    c = jnp.where(c >= lanes - HZ, c - lanes, c)
    fine = 2 * (r - bz // 2 * iz)
    spread = jnp.where((c == fine) | (c == fine + 1), 1.0, 0.0).astype(F32)

    window = coarse[pl.ds(cx * ix, n // 2)].reshape(n // 2 * crows, clanes)
    window = dot(window, spread).reshape(n // 2, crows, lanes)
    for i in range(n // 2):
        error = dot(split, window[i])
        field[2 * i] = start[2 * i] + error
        field[2 * i + 1] = start[2 * i + 1] + error
    coefs = (faces, over)
    low = HX - 2
    sweep(low, n - low, field, step, coefs, None, 1.0 / THETA)
    for turn, (keep, gain) in enumerate(chebyshev()):
        low = HX - 2 if turn == 0 else HX
        sweep(low, n - low, field, step, coefs, keep, gain)
    for i in range(bx):
        out[i] = field[HX + i, HY:HY + by, :bz]


def local(sizes, heat, material, table):
    nx, ny, nz = sizes
    bx, by, bz = heat.shape
    n, rows, lanes = bx + 2 * HX, by + 2 * HY, 2 * bz
    vmem = pl.BlockSpec(memory_space=pltpu.VMEM)
    smem = pl.BlockSpec(memory_space=pltpu.SMEM)
    limit = 30 * 1024 * 1024
    array = jax.ShapeDtypeStruct
    count = ny - 1 + nz - 1 + (nx - 1) * nz
    coarse = array((nx, nz, ny, bx // 4, by // 2, bz), F32)
    dma = pltpu.SemaphoreType.DMA
    ext, full_cond = pl.pallas_call(
        functools.partial(halo_kernel, sizes),
        out_shape=[array((2, n, rows, lanes), F32), coarse],
        in_specs=[vmem, vmem, smem],
        out_specs=[vmem, vmem],
        scratch_shapes=[
            pltpu.VMEM((2, 2, by, bz), F32),
            pltpu.VMEM((2, 2, rows, bz), F32),
            dma((8,)),
            dma((8,)),
            dma((count,)),
            dma((count,)),
        ],
        compiler_params=pltpu.CompilerParams(
            collective_id=0, has_side_effects=True, vmem_limit_bytes=limit
        ),
    )(heat, material, table)
    fine = pltpu.VMEM((n, rows, lanes), F32)
    faces, over, start, packed = pl.pallas_call(
        pre_kernel,
        out_shape=[
            array((6, n, rows, lanes), F32),
            array((n, rows, lanes), F32),
            array((n, rows, lanes), F32),
            array((bx // 4, by // 2, bz), F32),
        ],
        in_specs=[vmem],
        out_specs=[vmem] * 4,
        scratch_shapes=[fine] * 2 + [pltpu.VMEM((bx, by, bz), F32)],
        compiler_params=pltpu.CompilerParams(vmem_limit_bytes=limit),
    )(ext)
    full_right = pl.pallas_call(
        functools.partial(gather_kernel, sizes),
        out_shape=coarse,
        in_specs=[vmem],
        out_specs=vmem,
        scratch_shapes=[pltpu.SemaphoreType.DMA((count,)), pltpu.SemaphoreType.DMA((count,))],
        compiler_params=pltpu.CompilerParams(
            collective_id=1, has_side_effects=True, vmem_limit_bytes=limit
        ),
    )(packed)
    scratch = [fine] * 2
    for level in range(1, LEVELS + 1):
        shape = (bx * nx >> level, by * ny >> level, max(bz * nz >> level, 128))
        extra = HX if level == 1 else 1
        scratch += [pltpu.VMEM(shape, F32)] * 2
        scratch += [pltpu.VMEM((shape[0] + extra, *shape[1:]), F32)]
        scratch += [pltpu.VMEM(shape, F32)] * 2
        scratch += [pltpu.VMEM((6, *shape), F32)]
        scratch += [pltpu.VMEM(shape, F32)] * 2
    return pl.pallas_call(
        functools.partial(post_kernel, sizes),
        out_shape=array(heat.shape, F32),
        in_specs=[vmem] * 5,
        out_specs=vmem,
        scratch_shapes=scratch,
        compiler_params=pltpu.CompilerParams(vmem_limit_bytes=limit),
    )(faces, over, start, full_right, full_cond)


def with_halo(block, sides):
    for axis, dim in sides:
        count = lax.axis_size(axis)
        forward = [(i, i + 1) for i in range(count - 1)]
        backward = [(target, source) for source, target in forward]
        low = lax.ppermute(
            lax.slice_in_dim(block, block.shape[dim] - 1, None, axis=dim), axis, forward
        )
        high = lax.ppermute(lax.slice_in_dim(block, 0, 1, axis=dim), axis, backward)
        block = jnp.concatenate([low, block, high], axis=dim)
    return block


def neighbours(block):
    padded = with_halo(block, (("gx", 0), ("gy", 1), ("gz", 2)))
    return (
        padded[2:, 1:-1, 1:-1],
        padded[:-2, 1:-1, 1:-1],
        padded[1:-1, 2:, 1:-1],
        padded[1:-1, :-2, 1:-1],
        padded[1:-1, 1:-1, 2:],
        padded[1:-1, 1:-1, :-2],
    )


def large_smooth(right, start, faces, diag, scale):
    inverse = 1.0 / (scale * diag)
    if start is None:
        step = inverse * right / THETA
        field = step
    else:
        step = inverse * large_resid(right, start, faces, diag, scale) / THETA
        field = start + step
    for keep, gain in chebyshev():
        step = keep * step + gain * inverse * large_resid(right, field, faces, diag, scale)
        field = field + step
    return field


def large_resid(right, field, faces, diag, scale):
    total = sum(face * near for face, near in zip(faces, neighbours(field)))
    return right - scale * (diag * field - total)


def restrict(field):
    sx, sy, sz = field.shape
    return field.reshape(sx // 2, 2, sy // 2, 2, sz // 2, 2).mean(axis=(1, 3, 5))


def large_cycle(right, cond, level, scale):
    faces = []
    for other in neighbours(cond):
        other = jnp.where(other > 0.0, other, cond)
        faces.append(2.0 * cond * other / (cond + other))
    diag = sum(faces)
    field = large_smooth(right, None, faces, diag, scale)
    if level < LEVELS:
        resid = large_resid(right, field, faces, diag, scale)
        error = large_cycle(restrict(resid), restrict(cond), level + 1, scale * 0.25)
        for dim in range(3):
            error = jnp.repeat(error, 2, dim)
        field = field + error
    return large_smooth(right, field, faces, diag, scale)


def large(heat, material, table):
    cond = jnp.zeros(heat.shape, F32)
    for which in range(MATERIALS):
        cond = cond + jnp.where(material == which, table[which], 0.0)
    return large_cycle(heat, cond, 0, 1.0)


def solution(mesh):
    sizes = tuple(mesh.shape[axis] for axis in ("gx", "gy", "gz"))

    def run(heat, material, table):
        small = heat.size // 8 <= 1 << 18
        body = functools.partial(local, sizes) if small else large
        spec = P("gx", "gy", "gz")
        return jax.shard_map(
            body, mesh=mesh, in_specs=(spec, spec, P()), out_specs=spec, check_vma=False
        )(heat, material, table)

    return run
```
